32 devices in a mesh: dp: 4 (over y, x), mp: 8 (over z, core).
Axes of the slice: x: 2, y: 2, z: 4, core: 2. Of those that a mesh axis runs over, the one named last changes fastest.
Arguments:
- hidden_in: bfloat16 [512, 8192], P('dp', 'mp'), may hold values from -256 to 256
- out_grad: bfloat16 [512, 8192], P('dp', 'mp'), may hold values from -1.796875 to 1.796875
- neighbours: bfloat16 [80, 128, 1536], P('dp', 'mp'), may hold values from -6 to 6
- counts: int32 [8], P('dp'), may hold values from 2 to 10, as said below
- slot_owner: int32 [80], P('dp'), may hold values from -1 to 79, as said below
- w_query: bfloat16 [8192, 4096], P(None, 'mp'), may hold values from -0.0625 to 0.0625
- w_key: bfloat16 [1536, 4096], P(None, 'mp'), may hold values from -0.15625 to 0.15625
- w_value: bfloat16 [1536, 4096], P(None, 'mp'), may hold values from -0.15625 to 0.15625
- w_out: bfloat16 [4096, 8192], P('mp'), may hold values from -0.59765625 to 0.59765625
Outputs:
- layer_out: bfloat16 [512, 8192], P('dp', 'mp')
- neighbour_grad: bfloat16 [80, 128, 1536], P('dp', 'mp')
The draws below stay inside these ranges and needn't reach their ends.
Inputs may be any that keep to these rules, and one draw needn't show every extreme that they name: `counts`: every draw has one decoder group (spans g * 2 to g * 2 + 1) whose spans all have 10 neighbours. `slot_owner`: entry i is the span slot c * 10 + j that encoder slot i fills, or -1 for an empty encoder slot. Each slot with j < counts[c] is named exactly once, no other slot is named. The 20 entries of one index of dp name at most 5 slots of the spans of one decoder group (spans g * 2 to g * 2 + 1), and in every draw some index of dp names exactly 5 for some group.
All inputs are finite; a program needn't handle non-finite values.
Results may differ from the reference program's by a relative error of at most 0.024.
Values may be sent and summed in bfloat16 or wider, within the bound.
A program may use at most 128 MiB of HBM per device.

```python
import math
import jax
import jax.numpy as jnp
from jax import lax

D = 8192
HEADS = 32
DH = 128
ENC = 1536
CLEN = 64
NLEN = 128
MAXN = 10
CH = 2
QW = 4096
NCH = 8
TOKENS = 512
NEIGH = 80
N_MP = 8


def shuffled(sub_key, length):
    return jax.random.permutation(sub_key, length)


def neighbour_plan(key):
    key_count, key_group, key_source, key_shuffle = jax.random.split(key, 4)
    groups = NCH // CH
    capacity = (CH * MAXN + groups - 1) // groups
    counts = jax.random.randint(key_count, (NCH,), 2, MAXN + 1)
    full_group = jax.random.randint(key_group, (), 0, groups)
    span_group = jnp.arange(NCH) // CH
    counts = jnp.where(span_group == full_group, MAXN, counts).astype(jnp.int32)
    orders = jax.vmap(partial_perm(groups))(jax.random.split(key_source, groups))
    inverse = jnp.argsort(orders, axis=1)
    place = jnp.transpose(inverse)[:, :, None] * capacity + jnp.arange(capacity)[None, None, :]
    span_in = jnp.minimum(place // MAXN, CH - 1)
    slot_in = place % MAXN
    span_ids = jnp.arange(groups)[None, :, None] * CH + span_in
    valid = (place < CH * MAXN) & (slot_in < counts[span_ids])
    targets = jnp.where(valid, span_ids * MAXN + slot_in, -1).reshape(groups, groups * capacity)
    shuffles = jax.vmap(partial_perm(groups * capacity))(jax.random.split(key_shuffle, groups))
    owners = jnp.take_along_axis(targets, shuffles, axis=1).reshape(-1).astype(jnp.int32)
    return (counts, owners)


def partial_perm(length):

    def apply_perm(sub_key):
        return shuffled(sub_key, length)
    return apply_perm


def draw_counts(key, part):
    return neighbour_plan(key)[0]


def draw_slot_owner(key, part):
    return neighbour_plan(key)[1]


def draw_hidden_in(key, part):
    key = jax.random.fold_in(key, 11)
    key_base = jax.random.fold_in(key, 0)
    values = jnp.clip(jax.random.normal(key_base, (TOKENS, D), jnp.float32), -6.0, 6.0)
    return values.astype(jnp.bfloat16)


def shard_levels(own_key, extent, pieces, low, largest):
    level, own = 1.0, jax.random.fold_in(own_key, 6)
    for dim, shards_of in pieces:
        steps = jnp.exp(jax.random.uniform(jax.random.fold_in(own, dim), (shards_of,), jnp.float32, low / len(pieces), largest / len(pieces)))
        level = level * jnp.repeat(steps, extent[dim] // shards_of).reshape([-1 if axis == dim else 1 for axis in range(len(extent))])
    return level


def centred(key, shape, deviation, most, cuts=(), kind=jnp.bfloat16):
    drawn = jax.random.normal(key, shape, jnp.float32) * deviation
    if len(cuts) > 0:
        drawn = shard_levels(key, shape, cuts, -0.22, 0.18) * drawn
    return jnp.clip(drawn, min=-most, max=most).astype(kind)


def setup_inputs(seed: int = 0) -> dict:
    seeds = jax.random.split(jax.random.key(seed), 10)
    hidden_in = draw_hidden_in(jax.random.fold_in(seeds[9], 71), 0)
    out_grad = centred(seeds[1], (TOKENS, D), 0.3, 1.796875, ((0, 4), (1, 8)))
    neighbours = centred(seeds[2], (NEIGH, NLEN, ENC), 1.0, 6.0, ((0, 4), (1, 8)))
    counts = draw_counts(jax.random.fold_in(seeds[9], 71), 0)
    slot_owner = draw_slot_owner(jax.random.fold_in(seeds[9], 71), 0)
    w_query = centred(seeds[5], (D, QW), D ** -0.5, 0.0625, ((1, 8),))
    w_key = centred(seeds[6], (ENC, QW), ENC ** -0.5, 0.15625, ((1, 8),))
    w_value = centred(seeds[7], (ENC, QW), ENC ** -0.5, 0.15625, ((1, 8),))
    w_out = centred(seeds[8], (QW, D), 0.1, 0.59765625, ((0, 8),))
    return {"hidden_in": hidden_in, "out_grad": out_grad, "neighbours": neighbours, "counts": counts, "slot_owner": slot_owner, "w_query": w_query, "w_key": w_key, "w_value": w_value, "w_out": w_out}


def span_attention(queries, key_rows, value_rows, live_keys, grad_attended):
    score_scale = 1.0 / math.sqrt(DH)
    query_f = queries.astype(jnp.float32)
    key_f = key_rows.astype(jnp.float32)
    value_f = value_rows.astype(jnp.float32)
    grad_f = grad_attended.astype(jnp.float32)
    scores = jnp.einsum('qhd,khd->hqk', query_f, key_f) * score_scale
    scores = jnp.where(live_keys[None, None, :], scores, -jnp.inf)
    peak_score = lax.optimization_barrier(jnp.max(scores, axis=-1, keepdims=True))
    exponent = jnp.exp(scores - peak_score)
    weights = exponent / lax.optimization_barrier(jnp.sum(exponent, axis=-1, keepdims=True))
    weights_bf = weights.astype(jnp.bfloat16).astype(jnp.float32)
    attended = jnp.einsum('hqk,khd->qhd', weights_bf, value_f).astype(jnp.bfloat16)
    grad_values = jnp.einsum('hqk,qhd->khd', weights_bf, grad_f).astype(jnp.bfloat16)
    grad_weights = jnp.einsum('qhd,khd->hqk', grad_f, value_f)
    inner_sum = lax.optimization_barrier(jnp.sum(weights * grad_weights, axis=-1, keepdims=True))
    grad_scores = (weights * (grad_weights - inner_sum) * score_scale).astype(jnp.bfloat16)
    grad_keys = jnp.einsum('hqk,qhd->khd', grad_scores.astype(jnp.float32), query_f).astype(jnp.bfloat16)
    return (attended, grad_keys, grad_values)

def reference(hidden_in, out_grad, neighbours, counts, slot_owner, w_query, w_key, w_value, w_out):
    slot_ids = jnp.arange(NCH * MAXN, dtype=jnp.int32)
    matches = slot_owner[None, :] == slot_ids[:, None]
    encoder_ids = jnp.arange(NEIGH, dtype=jnp.int32)
    source = lax.optimization_barrier(jnp.sum(jnp.where(matches, encoder_ids[None, :], 0), axis=1)).astype(jnp.int32)
    gathered = jnp.take(neighbours, source, axis=0)
    queries = jnp.dot(hidden_in, w_query, preferred_element_type=jnp.float32).astype(jnp.bfloat16)
    grad_attended = lax.dot_general(out_grad, w_out, (((1,), (1,)), ((), ())), preferred_element_type=jnp.float32).astype(jnp.bfloat16)
    group_width = QW // N_MP

    def per_span(inputs):
        span_query, span_grad, span_neigh, span_count = inputs
        flat_rows = span_neigh.reshape(MAXN * NLEN, ENC)
        key_rows = jnp.dot(flat_rows, w_key, preferred_element_type=jnp.float32).astype(jnp.bfloat16)
        value_rows = jnp.dot(flat_rows, w_value, preferred_element_type=jnp.float32).astype(jnp.bfloat16)
        live_keys = jnp.arange(MAXN * NLEN, dtype=jnp.int32) // NLEN < span_count
        attended, grad_keys, grad_values = span_attention(span_query.reshape(CLEN, HEADS, DH), key_rows.reshape(MAXN * NLEN, HEADS, DH), value_rows.reshape(MAXN * NLEN, HEADS, DH), live_keys, span_grad.reshape(CLEN, HEADS, DH))
        grad_keys = grad_keys.reshape(MAXN * NLEN, QW)
        grad_values = grad_values.reshape(MAXN * NLEN, QW)
        running = jnp.zeros((MAXN * NLEN, ENC), jnp.float32)
        for shard in range(N_MP):
            low = shard * group_width
            high = low + group_width
            partial_value = lax.dot_general(grad_keys[:, low:high], w_key[:, low:high], (((1,), (1,)), ((), ())), preferred_element_type=jnp.float32)
            partial_value = partial_value + lax.dot_general(grad_values[:, low:high], w_value[:, low:high], (((1,), (1,)), ((), ())), preferred_element_type=jnp.float32)
            rounded = lax.optimization_barrier(partial_value.astype(jnp.bfloat16))
            running = running + rounded.astype(jnp.float32)
        return (attended.reshape(CLEN, QW), running.astype(jnp.bfloat16).reshape(MAXN, NLEN, ENC))
    attended, grad_slots = lax.map(per_span, (queries.reshape(NCH, CLEN, QW), grad_attended.reshape(NCH, CLEN, QW), gathered.reshape(NCH, MAXN, NLEN, ENC), counts))
    attended = attended.reshape(TOKENS, QW)
    running = jnp.zeros((TOKENS, D), jnp.float32)
    for shard in range(N_MP):
        low = shard * group_width
        high = low + group_width
        partial_value = jnp.dot(attended[:, low:high], w_out[low:high, :], preferred_element_type=jnp.float32)
        rounded = lax.optimization_barrier(partial_value.astype(jnp.bfloat16))
        running = running + rounded.astype(jnp.float32)
    layer_out = running.astype(jnp.bfloat16)
    grad_slots = grad_slots.reshape(NCH * MAXN, NLEN, ENC)
    picked = jnp.take(grad_slots, jnp.maximum(slot_owner, 0).astype(jnp.int32), axis=0)
    neighbour_grad = jnp.where((slot_owner >= 0)[:, None, None], picked, jnp.zeros_like(picked))
    return (layer_out, neighbour_grad)
```

```python
import functools
import math

import jax
import jax.numpy as jnp
from jax import lax
from jax.experimental import pallas as pl
from jax.experimental.pallas import tpu as pltpu
from jax.sharding import PartitionSpec as P

DH = 128
MAXN = 10
MESH = pl.DeviceIdType.MESH
NT = (((1,), (1,)), ((), ()))
TN = (((0,), (0,)), ((), ()))
VMEM_LIMIT = 62 * 1024 * 1024


def dot_f32(a, b, dims=(((1,), (0,)), ((), ()))):
    return lax.dot_general(a, b, dims, preferred_element_type=jnp.float32)


def greet(peers):
    barrier = pltpu.get_barrier_semaphore()
    total = 0
    for cond, dev in peers:
        if cond is None:
            pl.semaphore_signal(barrier, inc=1, device_id=dev, device_id_type=MESH)
            total = total + 1
        else:

            @pl.when(cond)
            def _(dev=dev):
                pl.semaphore_signal(barrier, inc=1, device_id=dev, device_id_type=MESH)

            total = total + jnp.where(cond, 1, 0)
    pl.semaphore_wait(barrier, total)


def forward_kernel(
    n_dp,
    n_mp,
    capacity,
    xd_in,
    rows_in,
    tags_in,
    counts_in,
    wq_in,
    wk_in,
    wv_in,
    wo_in,
    att_out,
    gk_out,
    gv_out,
    xd,
    nb,
    tags,
    wq,
    wk,
    wv,
    wo,
    keys,
    vals,
    queries,
    grads,
    bias,
    w_sem,
    a2a_send,
    a2a_recv,
    tag_send,
    tag_recv,
    own_sem,
    xd_send,
    xd_recv,
    nb_send,
    nb_recv,
):
    dp = lax.axis_index("dp")
    mp = lax.axis_index("mp")
    n_z = n_mp // 2
    z = mp // 2
    core = mp % 2
    partner = {"mp": mp + 1 - 2 * core}
    up = {"mp": lax.rem(mp + 2, n_mp)}
    down = {"mp": lax.rem(mp + n_mp - 2, n_mp)}
    has_up = z < n_z - 1
    has_down = z > 0
    block = nb.shape[1] // n_dp
    tokens = att_out.shape[0]
    feat = xd.shape[2]

    def peer(k):
        return lax.rem(dp + k, n_dp)

    weight_copies = [
        pltpu.make_async_copy(src, dst, w_sem.at[i])
        for i, (src, dst) in enumerate(((wq_in, wq), (wo_in, wo), (wk_in, wk), (wv_in, wv)))
    ]

    def line(buf, send, recv, origin, direction):
        slot = origin * 2 + core
        return pltpu.make_async_remote_copy(
            src_ref=buf.at[slot],
            dst_ref=buf.at[slot],
            send_sem=send.at[direction, origin],
            recv_sem=recv.at[slot],
            device_id=(up, down, partner)[direction],
            device_id_type=MESH,
        )

    def arrived(buf, send, recv, slot):
        pltpu.make_async_remote_copy(
            src_ref=buf.at[slot],
            dst_ref=buf.at[slot],
            send_sem=send.at[0, 0],
            recv_sem=recv.at[slot],
            device_id=partner,
            device_id_type=MESH,
        ).wait_recv()

    def send_own(args):
        @pl.when(has_up)
        def _():
            line(*args, z, 0).start()

        @pl.when(has_down)
        def _():
            line(*args, z, 1).start()

        line(*args, z, 2).start()

    def relay(args, s):
        @pl.when(z - s >= 0)
        def _():
            arrived(*args, (z - s) * 2 + core)

            @pl.when(has_up)
            def _():
                line(*args, z - s, 0).start()

            line(*args, z - s, 2).start()

        @pl.when(z + s <= n_z - 1)
        def _():
            arrived(*args, (z + s) * 2 + core)

            @pl.when(has_down)
            def _():
                line(*args, z + s, 1).start()

            line(*args, z + s, 2).start()

    def drain(args):
        def step(origin, carry):
            @pl.when(jnp.logical_and(origin <= z, has_up))
            def _():
                line(*args, origin, 0).wait_send()

            @pl.when(jnp.logical_and(origin >= z, has_down))
            def _():
                line(*args, origin, 1).wait_send()

            line(*args, origin, 2).wait_send()
            return carry

        lax.fori_loop(0, n_z, step, 0)

    xd_args = (xd, xd_send, xd_recv)
    nb_args = (nb, nb_send, nb_recv)

    own_xd = pltpu.make_async_copy(xd_in, xd.at[mp], own_sem.at[0])
    own_rows = pltpu.make_async_copy(
        rows_in.at[dp], nb.at[mp, pl.ds(dp * block, block)], own_sem.at[1]
    )
    own_tags = pltpu.make_async_copy(tags_in.at[dp], tags.at[dp], own_sem.at[2])
    own_xd.start()
    own_rows.start()
    own_tags.start()
    greet(
        [(None, {"dp": peer(k)}) for k in range(1, n_dp)]
        + [(None, partner), (has_up, up), (has_down, down)]
    )

    def row_copy(k):
        to = peer(k)
        return pltpu.make_async_remote_copy(
            src_ref=rows_in.at[to],
            dst_ref=nb.at[mp, pl.ds(dp * block, block)],
            send_sem=a2a_send.at[k],
            recv_sem=a2a_recv.at[k],
            device_id={"dp": to},
            device_id_type=MESH,
        )

    def tag_copy(k):
        to = peer(k)
        return pltpu.make_async_remote_copy(
            src_ref=tags_in.at[to],
            dst_ref=tags.at[dp],
            send_sem=tag_send.at[k],
            recv_sem=tag_recv.at[k],
            device_id={"dp": to},
            device_id_type=MESH,
        )

    for k in range(1, n_dp):
        row_copy(k).start()
    for k in range(1, n_dp):
        tag_copy(k).start()
    own_xd.wait()
    send_own(xd_args)
    for copy in weight_copies:
        copy.start()
    own_rows.wait()
    for k in range(1, n_dp):
        row_copy(k).wait()
    send_own(nb_args)
    own_tags.wait()
    for k in range(1, n_dp):
        tag_copy(k).wait()

    def xd_step(s, carry):
        relay(xd_args, s)
        return carry

    lax.fori_loop(1, n_z, xd_step, 0)

    def project(slot):
        rows = nb[slot]
        keys[slot] = dot_f32(rows, wk[...]).astype(jnp.bfloat16)
        vals[slot] = dot_f32(rows, wv[...]).astype(jnp.bfloat16)

    def both_cores(origin):
        arrived(*nb_args, origin * 2 + 1 - core)

        def step(c, carry):
            project(origin * 2 + c)
            return carry

        lax.fori_loop(0, 2, step, 0)

    def nb_step(s, carry):
        relay(nb_args, s)

        @pl.when(s == 1)
        def _():
            for copy in weight_copies:
                copy.wait()

            def other(origin, c):
                arrived(*xd_args, origin * 2 + 1 - core)
                return c

            lax.fori_loop(0, n_z, other, 0)

            def add(m, c):
                q, g = c
                cols = pl.ds(pl.multiple_of(m * feat, feat), feat)
                q = q + dot_f32(xd[m, :tokens, :], wq[cols, :])
                g = g + dot_f32(xd[m, tokens:, :], wo[:, cols], NT)
                return (q, g)

            zero = jnp.zeros(queries.shape, jnp.float32)
            q, g = lax.fori_loop(0, n_mp, add, (zero, zero))
            queries[...] = q.astype(jnp.bfloat16)
            grads[...] = g.astype(jnp.bfloat16)
            both_cores(z)

        @pl.when(z - s >= 0)
        def _():
            both_cores(z - s)

        @pl.when(z + s <= n_z - 1)
        def _():
            both_cores(z + s)

        return carry

    lax.fori_loop(1, n_z, nb_step, 0)

    span_len = tokens // (counts_in.shape[0])
    lane = lax.broadcasted_iota(jnp.int32, (1, tokens), 1)
    spans = counts_in.shape[0]
    first = jnp.zeros((1, tokens), jnp.int32)
    limit = jnp.zeros((1, tokens), jnp.int32)
    for c in range(spans):
        here = jnp.logical_and(lane >= c * span_len, lane < (c + 1) * span_len)
        first = jnp.where(here, (dp * spans + c) * MAXN, first)
        limit = jnp.where(here, counts_in[c : c + 1, :], limit)
    width = block // capacity
    for g in range(n_dp):
        for i in range(capacity):
            tag = tags[g, i : i + 1, :]
            place = tag - first
            live = jnp.logical_and(tag >= 0, jnp.logical_and(place >= 0, place < limit))
            value = jnp.where(live, 0.0, -jnp.inf)
            low = (g * capacity + i) * width
            bias[low : low + width, :] = jnp.broadcast_to(value, (width, tokens))

    scale = 1.0 / math.sqrt(DH)
    shard = nb.shape[1]
    total = n_mp * shard
    for h in range(queries.shape[1] // DH):
        cols = slice(h * DH, (h + 1) * DH)
        q = queries[:, cols]
        g = grads[:, cols]
        k = keys[:, :, cols].reshape(total, DH)
        v = vals[:, :, cols].reshape(total, DH)
        scores = dot_f32(k, q, NT) * scale
        scores = (scores.reshape(n_mp, shard, tokens) + bias[...][None]).reshape(total, tokens)
        peak = jnp.max(scores, axis=0, keepdims=True)
        expo = jnp.exp(scores - peak)
        weights = expo * (1.0 / jnp.sum(expo, axis=0, keepdims=True))
        weights_bf = weights.astype(jnp.bfloat16)
        att_out[:, cols] = dot_f32(weights_bf, v, TN).astype(jnp.bfloat16)
        gv_out[:, :, cols] = dot_f32(weights_bf, g).astype(jnp.bfloat16).reshape(n_mp, shard, DH)
        grad_w = dot_f32(v, g, NT)
        inner = jnp.sum(weights * grad_w, axis=0, keepdims=True)
        grad_s = (weights * (grad_w - inner) * scale).astype(jnp.bfloat16)
        gk_out[:, :, cols] = dot_f32(grad_s, q).astype(jnp.bfloat16).reshape(n_mp, shard, DH)

    drain(xd_args)
    drain(nb_args)


def forward(xd_shard, send_rows, send_tags, counts_rows, w_query, w_key, w_value, w_out, n_dp, n_mp):
    capacity = send_tags.shape[1]
    tokens = xd_shard.shape[0] // 2
    send_tags = jnp.broadcast_to(
        jnp.pad(send_tags, ((0, 0), (0, -capacity % 8)), constant_values=-1)[:, :, None],
        (n_dp, capacity + (-capacity % 8), tokens),
    )
    shard = n_dp * send_rows.shape[1]
    enc = send_rows.shape[2]
    width = w_query.shape[1]

    bf = jnp.bfloat16
    n_z = n_mp // 2
    hbm = pl.BlockSpec(memory_space=pl.ANY)
    vm = pl.BlockSpec(memory_space=pltpu.VMEM)
    dma = pltpu.SemaphoreType.DMA
    return pl.pallas_call(
        functools.partial(forward_kernel, n_dp, n_mp, capacity),
        out_shape=(
            jax.ShapeDtypeStruct((tokens, width), bf),
            jax.ShapeDtypeStruct((n_mp, shard, width), bf),
            jax.ShapeDtypeStruct((n_mp, shard, width), bf),
        ),
        in_specs=[hbm, hbm, hbm, vm, hbm, hbm, hbm, hbm],
        out_specs=(vm, vm, vm),
        scratch_shapes=[
            pltpu.VMEM((n_mp,) + xd_shard.shape, bf),
            pltpu.VMEM((n_mp, shard, enc), bf),
            pltpu.VMEM(send_tags.shape, jnp.int32),
            pltpu.VMEM(w_query.shape, bf),
            pltpu.VMEM(w_key.shape, bf),
            pltpu.VMEM(w_value.shape, bf),
            pltpu.VMEM(w_out.shape, bf),
            pltpu.VMEM((n_mp, shard, width), bf),
            pltpu.VMEM((n_mp, shard, width), bf),
            pltpu.VMEM((tokens, width), bf),
            pltpu.VMEM((tokens, width), bf),
            pltpu.VMEM((shard, tokens), jnp.float32),
            dma((4,)),
            dma((n_dp,)),
            dma((n_dp,)),
            dma((n_dp,)),
            dma((n_dp,)),
            dma((3,)),
            dma((3, n_z)),
            dma((n_mp,)),
            dma((3, n_z)),
            dma((n_mp,)),
        ],
        compiler_params=pltpu.CompilerParams(
            collective_id=0, has_side_effects=True, vmem_limit_bytes=VMEM_LIMIT
        ),
        name="gather_attend",
    )(xd_shard, send_rows, send_tags, counts_rows, w_query, w_key, w_value, w_out)


def per_device(hidden_in, out_grad, neighbours, counts, slot_owner, w_query, w_key, w_value, w_out):
    groups = lax.axis_size("dp")
    n_mp = lax.axis_size("mp")
    spans = counts.shape[0]
    slots_group = spans * MAXN
    src_slots = slot_owner.shape[0]
    capacity = src_slots // groups
    rows_dev = neighbours.shape[1]
    enc_width = neighbours.shape[2]
    query_width = w_query.shape[1]
    slot_order = jnp.arange(src_slots, dtype=jnp.int32)
    dest_group = jnp.where(slot_owner >= 0, slot_owner // slots_group, -1)
    earlier = (dest_group[None, :] == dest_group[:, None]) & (
        slot_order[None, :] < slot_order[:, None]
    )
    rank_in = jnp.sum(earlier.astype(jnp.int32), axis=1)
    position = jnp.where(slot_owner >= 0, dest_group * capacity + rank_in, -1)
    picked = position[None, :] == slot_order[:, None]
    source = jnp.sum(jnp.where(picked, slot_order[None, :], 0), axis=1)
    filled = jnp.any(picked, axis=1)
    send_rows = jnp.where(
        filled[:, None, None], jnp.take(neighbours, source, axis=0), jnp.zeros((), jnp.bfloat16)
    )
    send_rows = send_rows.reshape(groups, capacity * rows_dev, enc_width)
    send_tags = jnp.sum(
        jnp.where(picked, slot_owner[None, :] + 1, 0), axis=1
    ).reshape(groups, capacity) - 1
    counts_rows = jnp.broadcast_to(counts[:, None], (spans, hidden_in.shape[0]))
    attended, grad_keys, grad_values = forward(
        jnp.concatenate([hidden_in, out_grad], axis=0),
        send_rows,
        send_tags,
        counts_rows,
        w_query,
        w_key,
        w_value,
        w_out,
        groups,
        n_mp,
    )
    grad_enc = lax.dot_general(
        grad_keys.reshape(-1, query_width), w_key, NT, preferred_element_type=jnp.float32
    )
    grad_enc = grad_enc + lax.dot_general(
        grad_values.reshape(-1, query_width), w_value, NT, preferred_element_type=jnp.float32
    )
    out_part = jnp.dot(attended, w_out, preferred_element_type=jnp.float32)
    grad_rows = lax.psum_scatter(
        grad_enc.astype(jnp.bfloat16), "mp", scatter_dimension=0, tiled=True
    )
    layer_out = lax.psum_scatter(
        out_part.astype(jnp.bfloat16), "mp", scatter_dimension=1, tiled=True
    )
    returned = lax.all_to_all(
        grad_rows.reshape(groups, capacity, rows_dev, enc_width),
        "dp",
        split_axis=0,
        concat_axis=0,
        tiled=True,
    )
    returned = returned.reshape(src_slots, rows_dev, enc_width)
    neighbour_grad = jnp.where(
        (slot_owner >= 0)[:, None, None],
        jnp.take(returned, jnp.maximum(position, 0), axis=0),
        jnp.zeros((), jnp.bfloat16),
    )
    return (layer_out, neighbour_grad)


def solution(mesh):
    return jax.shard_map(
        per_device,
        mesh=mesh,
        in_specs=(
            P("dp", "mp"),
            P("dp", "mp"),
            P("dp", "mp", None),
            P("dp"),
            P("dp"),
            P(None, "mp"),
            P(None, "mp"),
            P(None, "mp"),
            P("mp", None),
        ),
        out_specs=(P("dp", "mp"), P("dp", "mp", None)),
        check_vma=False,
    )
```

```python
import functools
import math

import jax
import jax.numpy as jnp
from jax import lax
from jax.experimental import pallas as pl
from jax.experimental.pallas import tpu as pltpu
from jax.sharding import PartitionSpec as P

DH = 128
MAXN = 10
MESH = pl.DeviceIdType.MESH
NT = (((1,), (1,)), ((), ()))
TN = (((0,), (0,)), ((), ()))
VMEM_LIMIT = 62 * 1024 * 1024


def dot_f32(a, b, dims=(((1,), (0,)), ((), ()))):
    return lax.dot_general(a, b, dims, preferred_element_type=jnp.float32)


def greet(peers):
    barrier = pltpu.get_barrier_semaphore()
    total = 0
    for cond, dev in peers:
        if cond is None:
            pl.semaphore_signal(barrier, inc=1, device_id=dev, device_id_type=MESH)
            total = total + 1
        else:

            @pl.when(cond)
            def _(dev=dev):
                pl.semaphore_signal(barrier, inc=1, device_id=dev, device_id_type=MESH)

            total = total + jnp.where(cond, 1, 0)
    pl.semaphore_wait(barrier, total)


def forward_kernel(
    n_dp,
    n_mp,
    capacity,
    xd_in,
    rows_in,
    tags_in,
    counts_in,
    wq_in,
    wk_in,
    wv_in,
    wo_in,
    att_out,
    gk_out,
    gv_out,
    xd,
    nb,
    tags,
    wq,
    wk,
    wv,
    wo,
    keys,
    vals,
    queries,
    grads,
    bias,
    w_sem,
    a2a_send,
    a2a_recv,
    tag_send,
    tag_recv,
    own_sem,
    xd_send,
    xd_recv,
    nb_send,
    nb_recv,
):
    dp = lax.axis_index("dp")
    mp = lax.axis_index("mp")
    n_z = n_mp // 2
    z = mp // 2
    core = mp % 2
    partner = {"mp": mp + 1 - 2 * core}
    up = {"mp": lax.rem(mp + 2, n_mp)}
    down = {"mp": lax.rem(mp + n_mp - 2, n_mp)}
    has_up = z < n_z - 1
    has_down = z > 0
    block = nb.shape[1] // n_dp
    tokens = att_out.shape[0]
    feat = xd.shape[2]

    def peer(k):
        return lax.rem(dp + k, n_dp)

    weight_copies = [
        pltpu.make_async_copy(src, dst, w_sem.at[i])
        for i, (src, dst) in enumerate(((wq_in, wq), (wo_in, wo), (wk_in, wk), (wv_in, wv)))
    ]

    def line(buf, send, recv, origin, direction):
        slot = origin * 2 + core
        return pltpu.make_async_remote_copy(
            src_ref=buf.at[slot],
            dst_ref=buf.at[slot],
            send_sem=send.at[direction, origin],
            recv_sem=recv.at[slot],
            device_id=(up, down, partner)[direction],
            device_id_type=MESH,
        )

    def arrived(buf, send, recv, slot):
        pltpu.make_async_remote_copy(
            src_ref=buf.at[slot],
            dst_ref=buf.at[slot],
            send_sem=send.at[0, 0],
            recv_sem=recv.at[slot],
            device_id=partner,
            device_id_type=MESH,
        ).wait_recv()

    def send_own(args):
        @pl.when(has_up)
        def _():
            line(*args, z, 0).start()

        @pl.when(has_down)
        def _():
            line(*args, z, 1).start()

        line(*args, z, 2).start()

    def relay(args, s):
        @pl.when(z - s >= 0)
        def _():
            arrived(*args, (z - s) * 2 + core)

            @pl.when(has_up)
            def _():
                line(*args, z - s, 0).start()

            line(*args, z - s, 2).start()

        @pl.when(z + s <= n_z - 1)
        def _():
            arrived(*args, (z + s) * 2 + core)

            @pl.when(has_down)
            def _():
                line(*args, z + s, 1).start()

            line(*args, z + s, 2).start()

    def drain(args):
        def step(origin, carry):
            @pl.when(jnp.logical_and(origin <= z, has_up))
            def _():
                line(*args, origin, 0).wait_send()

            @pl.when(jnp.logical_and(origin >= z, has_down))
            def _():
                line(*args, origin, 1).wait_send()

            line(*args, origin, 2).wait_send()
            return carry

        lax.fori_loop(0, n_z, step, 0)

    xd_args = (xd, xd_send, xd_recv)
    nb_args = (nb, nb_send, nb_recv)

    own_xd = pltpu.make_async_copy(xd_in, xd.at[mp], own_sem.at[0])
    own_rows = pltpu.make_async_copy(
        rows_in.at[dp], nb.at[mp, pl.ds(dp * block, block)], own_sem.at[1]
    )
    own_tags = pltpu.make_async_copy(tags_in.at[dp], tags.at[dp], own_sem.at[2])
    own_xd.start()
    own_rows.start()
    own_tags.start()
    greet(
        [(None, {"dp": peer(k)}) for k in range(1, n_dp)]
        + [(None, partner), (has_up, up), (has_down, down)]
    )

    def row_copy(k):
        to = peer(k)
        return pltpu.make_async_remote_copy(
            src_ref=rows_in.at[to],
            dst_ref=nb.at[mp, pl.ds(dp * block, block)],
            send_sem=a2a_send.at[k],
            recv_sem=a2a_recv.at[k],
            device_id={"dp": to},
            device_id_type=MESH,
        )

    def tag_copy(k):
        to = peer(k)
        return pltpu.make_async_remote_copy(
            src_ref=tags_in.at[to],
            dst_ref=tags.at[dp],
            send_sem=tag_send.at[k],
            recv_sem=tag_recv.at[k],
            device_id={"dp": to},
            device_id_type=MESH,
        )

    for k in range(1, n_dp):
        row_copy(k).start()
    for k in range(1, n_dp):
        tag_copy(k).start()
    own_xd.wait()
    send_own(xd_args)
    for copy in weight_copies:
        copy.start()
    own_rows.wait()
    for k in range(1, n_dp):
        row_copy(k).wait()
    send_own(nb_args)
    own_tags.wait()
    for k in range(1, n_dp):
        tag_copy(k).wait()

    def xd_step(s, carry):
        relay(xd_args, s)
        return carry

    lax.fori_loop(1, n_z, xd_step, 0)

    def project(slot):
        rows = nb[slot]
        keys[slot] = dot_f32(rows, wk[...]).astype(jnp.bfloat16)
        vals[slot] = dot_f32(rows, wv[...]).astype(jnp.bfloat16)

    def both_cores(origin):
        arrived(*nb_args, origin * 2 + 1 - core)

        def step(c, carry):
            project(origin * 2 + c)
            return carry

        lax.fori_loop(0, 2, step, 0)

    def nb_step(s, carry):
        relay(nb_args, s)

        @pl.when(s == 1)
        def _():
            for copy in weight_copies:
                copy.wait()

            def other(origin, c):
                arrived(*xd_args, origin * 2 + 1 - core)
                return c

            lax.fori_loop(0, n_z, other, 0)

            def add(m, c):
                q, g = c
                cols = pl.ds(pl.multiple_of(m * feat, feat), feat)
                q = q + dot_f32(xd[m, :tokens, :], wq[cols, :])
                g = g + dot_f32(xd[m, tokens:, :], wo[:, cols], NT)
                return (q, g)

            zero = jnp.zeros(queries.shape, jnp.float32)
            q, g = lax.fori_loop(0, n_mp, add, (zero, zero))
            queries[...] = q.astype(jnp.bfloat16)
            grads[...] = g.astype(jnp.bfloat16)
            both_cores(z)

        @pl.when(z - s >= 0)
        def _():
            both_cores(z - s)

        @pl.when(z + s <= n_z - 1)
        def _():
            both_cores(z + s)

        return carry

    lax.fori_loop(1, n_z, nb_step, 0)

    span_len = tokens // (counts_in.shape[0])
    lane = lax.broadcasted_iota(jnp.int32, (1, tokens), 1)
    spans = counts_in.shape[0]
    first = jnp.zeros((1, tokens), jnp.int32)
    limit = jnp.zeros((1, tokens), jnp.int32)
    for c in range(spans):
        here = jnp.logical_and(lane >= c * span_len, lane < (c + 1) * span_len)
        first = jnp.where(here, (dp * spans + c) * MAXN, first)
        limit = jnp.where(here, counts_in[c : c + 1, :], limit)
    width = block // capacity
    for g in range(n_dp):
        for i in range(capacity):
            tag = tags[g, i : i + 1, :]
            place = tag - first
            live = jnp.logical_and(tag >= 0, jnp.logical_and(place >= 0, place < limit))
            value = jnp.where(live, 0.0, -jnp.inf)
            low = (g * capacity + i) * width
            bias[low : low + width, :] = jnp.broadcast_to(value, (width, tokens))

    scale = 1.0 / math.sqrt(DH)
    shard = nb.shape[1]
    total = n_mp * shard
    for h in range(queries.shape[1] // DH):
        cols = slice(h * DH, (h + 1) * DH)
        q = queries[:, cols]
        g = grads[:, cols]
        k = keys[:, :, cols].reshape(total, DH)
        v = vals[:, :, cols].reshape(total, DH)
        scores = dot_f32(k, q, NT) * scale
        scores = (scores.reshape(n_mp, shard, tokens) + bias[...][None]).reshape(total, tokens)
        peak = jnp.max(scores, axis=0, keepdims=True)
        expo = jnp.exp(scores - peak)
        weights = expo * (1.0 / jnp.sum(expo, axis=0, keepdims=True))
        weights_bf = weights.astype(jnp.bfloat16)
        att_out[:, cols] = dot_f32(weights_bf, v, TN).astype(jnp.bfloat16)
        gv_out[:, :, cols] = dot_f32(weights_bf, g).astype(jnp.bfloat16).reshape(n_mp, shard, DH)
        grad_w = dot_f32(v, g, NT)
        inner = jnp.sum(weights * grad_w, axis=0, keepdims=True)
        grad_s = (weights * (grad_w - inner) * scale).astype(jnp.bfloat16)
        gk_out[:, :, cols] = dot_f32(grad_s, q).astype(jnp.bfloat16).reshape(n_mp, shard, DH)

    drain(xd_args)
    drain(nb_args)


def forward(xd_shard, send_rows, send_tags, counts_rows, w_query, w_key, w_value, w_out, n_dp, n_mp):
    capacity = send_tags.shape[1]
    tokens = xd_shard.shape[0] // 2
    send_tags = jnp.broadcast_to(
        jnp.pad(send_tags, ((0, 0), (0, -capacity % 8)), constant_values=-1)[:, :, None],
        (n_dp, capacity + (-capacity % 8), tokens),
    )
    shard = n_dp * send_rows.shape[1]
    enc = send_rows.shape[2]
    width = w_query.shape[1]

    bf = jnp.bfloat16
    n_z = n_mp // 2
    hbm = pl.BlockSpec(memory_space=pl.ANY)
    vm = pl.BlockSpec(memory_space=pltpu.VMEM)
    dma = pltpu.SemaphoreType.DMA
    return pl.pallas_call(
        functools.partial(forward_kernel, n_dp, n_mp, capacity),
        out_shape=(
            jax.ShapeDtypeStruct((tokens, width), bf),
            jax.ShapeDtypeStruct((n_mp, shard, width), bf),
            jax.ShapeDtypeStruct((n_mp, shard, width), bf),
        ),
        in_specs=[hbm, hbm, hbm, vm, hbm, hbm, hbm, hbm],
        out_specs=(vm, vm, vm),
        scratch_shapes=[
            pltpu.VMEM((n_mp,) + xd_shard.shape, bf),
            pltpu.VMEM((n_mp, shard, enc), bf),
            pltpu.VMEM(send_tags.shape, jnp.int32),
            pltpu.VMEM(w_query.shape, bf),
            pltpu.VMEM(w_key.shape, bf),
            pltpu.VMEM(w_value.shape, bf),
            pltpu.VMEM(w_out.shape, bf),
            pltpu.VMEM((n_mp, shard, width), bf),
            pltpu.VMEM((n_mp, shard, width), bf),
            pltpu.VMEM((tokens, width), bf),
            pltpu.VMEM((tokens, width), bf),
            pltpu.VMEM((shard, tokens), jnp.float32),
            dma((4,)),
            dma((n_dp,)),
            dma((n_dp,)),
            dma((n_dp,)),
            dma((n_dp,)),
            dma((3,)),
            dma((3, n_z)),
            dma((n_mp,)),
            dma((3, n_z)),
            dma((n_mp,)),
        ],
        compiler_params=pltpu.CompilerParams(
            collective_id=0, has_side_effects=True, vmem_limit_bytes=VMEM_LIMIT
        ),
        name="gather_attend",
    )(xd_shard, send_rows, send_tags, counts_rows, w_query, w_key, w_value, w_out)


def backward_kernel(
    n_dp,
    n_mp,
    att,
    gk,
    gv,
    wk_in,
    wv_in,
    wo_in,
    layer_out,
    returned,
    wk,
    wv,
    wo,
    mine,
    theirs,
    paired,
    landed,
    out_mine,
    out_theirs,
    out_paired,
    out_landed,
    w_sem,
    pair_send,
    pair_recv,
    out_pair_send,
    out_pair_recv,
    hop_send,
    hop_recv,
    out_send,
    out_recv,
    a2a_send,
    a2a_recv,
    own_sem,
):
    dp = lax.axis_index("dp")
    mp = lax.axis_index("mp")
    n_z = n_mp // 2
    z = mp // 2
    core = mp % 2
    partner = {"mp": mp + 1 - 2 * core}
    up = {"mp": lax.rem(mp + 2, n_mp)}
    down = {"mp": lax.rem(mp + n_mp - 2, n_mp)}
    has_up = z < n_z - 1
    has_down = z > 0
    chunk = mine.shape[1] // n_dp
    feat = out_mine.shape[2]
    bf = jnp.bfloat16

    weight_copies = [
        pltpu.make_async_copy(src, dst, w_sem.at[i])
        for i, (src, dst) in enumerate(((wk_in, wk), (wv_in, wv), (wo_in, wo)))
    ]
    for copy in weight_copies:
        copy.start()
    greet(
        [(None, {"dp": lax.rem(dp + k, n_dp)}) for k in range(1, n_dp)]
        + [(None, partner), (has_up, up), (has_down, down)]
    )
    for copy in weight_copies:
        copy.wait()

    def pair_copy(d):
        return pltpu.make_async_remote_copy(
            src_ref=theirs.at[d],
            dst_ref=paired.at[d],
            send_sem=pair_send.at[d],
            recv_sem=pair_recv.at[d],
            device_id=partner,
            device_id_type=MESH,
        )

    def out_pair_copy(d):
        return pltpu.make_async_remote_copy(
            src_ref=out_theirs.at[d],
            dst_ref=out_paired.at[d],
            send_sem=out_pair_send.at[d],
            recv_sem=out_pair_recv.at[d],
            device_id=partner,
            device_id_type=MESH,
        )

    def grad_part(m):
        return (dot_f32(gk[m], wk[...], NT) + dot_f32(gv[m], wv[...], NT)).astype(bf)

    def out_part(m):
        cols = pl.ds(pl.multiple_of(m * feat, feat), feat)
        return dot_f32(att[...], wo[:, cols]).astype(bf)

    def add(a, b):
        return (a.astype(jnp.float32) + b.astype(jnp.float32)).astype(bf)

    def prepare(d):
        own, other = d * 2 + core, d * 2 + 1 - core
        theirs[d] = grad_part(other)
        pair_copy(d).start()
        out_theirs[d] = out_part(other)
        out_pair_copy(d).start()
        mine[d] = grad_part(own)
        out_mine[d] = out_part(own)
        pair_copy(d).wait()
        mine[d] = add(mine[d], paired[d])
        out_pair_copy(d).wait()
        out_mine[d] = add(out_mine[d], out_paired[d])

    def target(direction, k):
        j = k // n_dp
        return n_z - 1 - j if direction == 0 else j

    def slot_of(direction, d):
        return d if direction == 0 else jnp.where(d == z - 1, n_z, d)

    def hop(direction, k):
        d = target(direction, k)
        rows = pl.ds(pl.multiple_of((k % n_dp) * chunk, chunk), chunk)
        slot = slot_of(direction, d)
        return pltpu.make_async_remote_copy(
            src_ref=mine.at[d, rows],
            dst_ref=landed.at[slot, rows],
            send_sem=hop_send.at[direction, k],
            recv_sem=hop_recv.at[slot, k % n_dp],
            device_id=(up, down)[direction],
            device_id_type=MESH,
        )

    def hop_arrived(slot, g):
        rows = pl.ds(pl.multiple_of(g * chunk, chunk), chunk)
        pltpu.make_async_remote_copy(
            src_ref=landed.at[slot, rows],
            dst_ref=landed.at[slot, rows],
            send_sem=hop_send.at[0, 0],
            recv_sem=hop_recv.at[slot, g],
            device_id=partner,
            device_id_type=MESH,
        ).wait_recv()
        return rows

    def out_hop(direction, j):
        d = n_z - 1 - j if direction == 0 else j
        slot = slot_of(direction, d)
        return pltpu.make_async_remote_copy(
            src_ref=out_mine.at[d],
            dst_ref=out_landed.at[slot],
            send_sem=out_send.at[direction, j],
            recv_sem=out_recv.at[slot],
            device_id=(up, down)[direction],
            device_id_type=MESH,
        )

    def out_arrived(slot):
        pltpu.make_async_remote_copy(
            src_ref=out_landed.at[slot],
            dst_ref=out_landed.at[slot],
            send_sem=out_send.at[0, 0],
            recv_sem=out_recv.at[slot],
            device_id=partner,
            device_id_type=MESH,
        ).wait_recv()

    sent = (n_z - 1 - z, z)
    from_behind = (has_down, has_up)

    def step(s, carry):
        items = []
        for direction in range(2):
            j = s - (z if direction == 0 else n_z - 1 - z)
            d = n_z - 1 - j if direction == 0 else j
            active = jnp.logical_and(j >= 0, j < sent[direction])
            items.append((direction, j, d, active))

            @pl.when(active)
            def _(d=d):
                prepare(d)

        for direction, j, d, active in items:

            @pl.when(active)
            def _(direction=direction, j=j, d=d):
                @pl.when(from_behind[direction])
                def _():
                    out_arrived(d)
                    out_mine[d] = add(out_mine[d], out_landed[d])

                out_hop(direction, j).start()

        def each(g, c):
            for direction, j, d, active in items:

                @pl.when(active)
                def _(direction=direction, j=j, d=d):
                    @pl.when(from_behind[direction])
                    def _():
                        rows = hop_arrived(d, g)
                        mine[d, rows, :] = add(mine[d, rows, :], landed[d, rows, :])

                    k = j * n_dp + g

                    @pl.when(k >= 2)
                    def _():
                        hop(direction, k - 2).wait_send()

                    hop(direction, k).start()

            return c

        lax.fori_loop(0, n_dp, each, 0)
        return carry

    lax.fori_loop(0, n_z - 1, step, 0)

    prepare(z)

    @pl.when(has_down)
    def _():
        out_arrived(z)
        out_mine[z] = add(out_mine[z], out_landed[z])

    @pl.when(has_up)
    def _():
        out_arrived(n_z)
        out_mine[z] = add(out_mine[z], out_landed[n_z])

    layer_out[...] = out_mine[z]

    def back(g):
        rows = pl.ds(pl.multiple_of(g * chunk, chunk), chunk)
        return pltpu.make_async_remote_copy(
            src_ref=mine.at[z, rows],
            dst_ref=returned.at[dp],
            send_sem=a2a_send.at[g],
            recv_sem=a2a_recv.at[dp],
            device_id={"dp": g},
            device_id_type=MESH,
        )

    def back_arrived(g):
        rows = pl.ds(pl.multiple_of(g * chunk, chunk), chunk)
        pltpu.make_async_remote_copy(
            src_ref=mine.at[z, rows],
            dst_ref=returned.at[g],
            send_sem=a2a_send.at[g],
            recv_sem=a2a_recv.at[g],
            device_id={"dp": g},
            device_id_type=MESH,
        ).wait_recv()

    own_rows = pl.ds(pl.multiple_of(dp * chunk, chunk), chunk)
    own_copy = pltpu.make_async_copy(mine.at[z, own_rows], returned.at[dp], own_sem)

    def last(g, c):
        rows = pl.ds(pl.multiple_of(g * chunk, chunk), chunk)

        @pl.when(has_down)
        def _():
            hop_arrived(z, g)
            mine[z, rows, :] = add(mine[z, rows, :], landed[z, rows, :])

        @pl.when(has_up)
        def _():
            hop_arrived(n_z, g)
            mine[z, rows, :] = add(mine[z, rows, :], landed[n_z, rows, :])

        @pl.when(g != dp)
        def _():
            back(g).start()

        @pl.when(g == dp)
        def _():
            own_copy.start()

        return c

    lax.fori_loop(0, n_dp, last, 0)
    own_copy.wait()

    def finish(g, c):
        @pl.when(g != dp)
        def _():
            back(g).wait_send()
            back_arrived(g)

        return c

    lax.fori_loop(0, n_dp, finish, 0)

    for direction in range(2):

        @pl.when(sent[direction] > 0)
        def _(direction=direction):
            count = sent[direction] * n_dp
            hop(direction, count - 2).wait_send()
            hop(direction, count - 1).wait_send()

        def drain(j, c, direction=direction):
            @pl.when(j < sent[direction])
            def _():
                out_hop(direction, j).wait_send()

            return c

        lax.fori_loop(0, n_z - 1, drain, 0)


def backward(att, gk, gv, w_key, w_value, w_out, n_dp, n_mp):
    tokens = att.shape[0]
    shard = gk.shape[1]
    enc = w_key.shape[0]
    feat = w_out.shape[1] // n_mp
    n_z = n_mp // 2
    bf = jnp.bfloat16
    hbm = pl.BlockSpec(memory_space=pl.ANY)
    vm = pl.BlockSpec(memory_space=pltpu.VMEM)
    dma = pltpu.SemaphoreType.DMA
    return pl.pallas_call(
        functools.partial(backward_kernel, n_dp, n_mp),
        out_shape=(
            jax.ShapeDtypeStruct((tokens, feat), bf),
            jax.ShapeDtypeStruct((n_dp, shard // n_dp, enc), bf),
        ),
        in_specs=[vm, vm, vm, hbm, hbm, hbm],
        out_specs=(vm, hbm),
        scratch_shapes=[
            pltpu.VMEM(w_key.shape, bf),
            pltpu.VMEM(w_value.shape, bf),
            pltpu.VMEM(w_out.shape, bf),
            pltpu.VMEM((n_z, shard, enc), bf),
            pltpu.VMEM((n_z, shard, enc), bf),
            pltpu.VMEM((n_z, shard, enc), bf),
            pltpu.VMEM((n_z + 1, shard, enc), bf),
            pltpu.VMEM((n_z, tokens, feat), bf),
            pltpu.VMEM((n_z, tokens, feat), bf),
            pltpu.VMEM((n_z, tokens, feat), bf),
            pltpu.VMEM((n_z + 1, tokens, feat), bf),
            dma((3,)),
            dma((n_z,)),
            dma((n_z,)),
            dma((n_z,)),
            dma((n_z,)),
            dma((2, n_z * n_dp)),
            dma((n_z + 1, n_dp)),
            dma((2, n_z)),
            dma((n_z + 1,)),
            dma((n_dp,)),
            dma((n_dp,)),
            dma,
        ],
        compiler_params=pltpu.CompilerParams(
            collective_id=1, has_side_effects=True, vmem_limit_bytes=VMEM_LIMIT
        ),
        name="grads_scatter",
    )(att, gk, gv, w_key, w_value, w_out)


def per_device(hidden_in, out_grad, neighbours, counts, slot_owner, w_query, w_key, w_value, w_out):
    groups = lax.axis_size("dp")
    n_mp = lax.axis_size("mp")
    spans = counts.shape[0]
    slots_group = spans * MAXN
    src_slots = slot_owner.shape[0]
    capacity = src_slots // groups
    rows_dev = neighbours.shape[1]
    enc_width = neighbours.shape[2]
    slot_order = jnp.arange(src_slots, dtype=jnp.int32)
    dest_group = jnp.where(slot_owner >= 0, slot_owner // slots_group, -1)
    earlier = (dest_group[None, :] == dest_group[:, None]) & (
        slot_order[None, :] < slot_order[:, None]
    )
    rank_in = jnp.sum(earlier.astype(jnp.int32), axis=1)
    position = jnp.where(slot_owner >= 0, dest_group * capacity + rank_in, -1)
    picked = position[None, :] == slot_order[:, None]
    source = jnp.sum(jnp.where(picked, slot_order[None, :], 0), axis=1)
    filled = jnp.any(picked, axis=1)
    send_rows = jnp.where(
        filled[:, None, None], jnp.take(neighbours, source, axis=0), jnp.zeros((), jnp.bfloat16)
    )
    send_rows = send_rows.reshape(groups, capacity * rows_dev, enc_width)
    send_tags = jnp.sum(
        jnp.where(picked, slot_owner[None, :] + 1, 0), axis=1
    ).reshape(groups, capacity) - 1
    counts_rows = jnp.broadcast_to(counts[:, None], (spans, hidden_in.shape[0]))
    attended, grad_keys, grad_values = forward(
        jnp.concatenate([hidden_in, out_grad], axis=0),
        send_rows,
        send_tags,
        counts_rows,
        w_query,
        w_key,
        w_value,
        w_out,
        groups,
        n_mp,
    )
    layer_out, returned = backward(
        attended, grad_keys, grad_values, w_key, w_value, w_out, groups, n_mp
    )
    returned = returned.reshape(src_slots, rows_dev, enc_width)
    neighbour_grad = jnp.where(
        (slot_owner >= 0)[:, None, None],
        jnp.take(returned, jnp.maximum(position, 0), axis=0),
        jnp.zeros((), jnp.bfloat16),
    )
    return (layer_out, neighbour_grad)


def solution(mesh):
    return jax.shard_map(
        per_device,
        mesh=mesh,
        in_specs=(
            P("dp", "mp"),
            P("dp", "mp"),
            P("dp", "mp", None),
            P("dp"),
            P("dp"),
            P(None, "mp"),
            P(None, "mp"),
            P(None, "mp"),
            P("mp", None),
        ),
        out_specs=(P("dp", "mp"), P("dp", "mp", None)),
        check_vma=False,
    )
```

```python
import functools
import math

import jax
import jax.numpy as jnp
from jax import lax
from jax.experimental import pallas as pl
from jax.experimental.pallas import tpu as pltpu
from jax.sharding import PartitionSpec as P

DH = 128
MAXN = 10
MESH = pl.DeviceIdType.MESH
NT = (((1,), (1,)), ((), ()))
TN = (((0,), (0,)), ((), ()))
VMEM_LIMIT = 62 * 1024 * 1024


def dot_f32(a, b, dims=(((1,), (0,)), ((), ()))):
    return lax.dot_general(a, b, dims, preferred_element_type=jnp.float32)


def greet(peers):
    barrier = pltpu.get_barrier_semaphore()
    total = 0
    for cond, dev in peers:
        if cond is None:
            pl.semaphore_signal(barrier, inc=1, device_id=dev, device_id_type=MESH)
            total = total + 1
        else:

            @pl.when(cond)
            def _(dev=dev):
                pl.semaphore_signal(barrier, inc=1, device_id=dev, device_id_type=MESH)

            total = total + jnp.where(cond, 1, 0)
    pl.semaphore_wait(barrier, total)


def forward_kernel(
    n_dp,
    n_mp,
    capacity,
    xd_in,
    rows_in,
    tags_in,
    counts_in,
    wq_in,
    wk_in,
    wv_in,
    wo_in,
    att_out,
    gk_out,
    gv_out,
    xd,
    nb,
    tags,
    wq,
    wk,
    wv,
    wo,
    scores,
    grad_w,
    vals,
    queries,
    grads,
    bias,
    w_sem,
    a2a_send,
    a2a_recv,
    tag_send,
    tag_recv,
    own_sem,
    xd_send,
    xd_recv,
    nb_send,
    nb_recv,
):
    dp = lax.axis_index("dp")
    mp = lax.axis_index("mp")
    n_z = n_mp // 2
    z = mp // 2
    core = mp % 2
    partner = {"mp": mp + 1 - 2 * core}
    up = {"mp": lax.rem(mp + 2, n_mp)}
    down = {"mp": lax.rem(mp + n_mp - 2, n_mp)}
    has_up = z < n_z - 1
    has_down = z > 0
    block = nb.shape[1] // n_dp
    tokens = att_out.shape[0]
    feat = xd.shape[2]

    def peer(k):
        return lax.rem(dp + k, n_dp)

    weight_copies = [
        pltpu.make_async_copy(src, dst, w_sem.at[i])
        for i, (src, dst) in enumerate(((wq_in, wq), (wo_in, wo), (wk_in, wk), (wv_in, wv)))
    ]

    def line(buf, send, recv, origin, direction):
        slot = origin * 2 + core
        return pltpu.make_async_remote_copy(
            src_ref=buf.at[slot],
            dst_ref=buf.at[slot],
            send_sem=send.at[direction, origin],
            recv_sem=recv.at[slot],
            device_id=(up, down, partner)[direction],
            device_id_type=MESH,
        )

    def arrived(buf, send, recv, slot):
        pltpu.make_async_remote_copy(
            src_ref=buf.at[slot],
            dst_ref=buf.at[slot],
            send_sem=send.at[0, 0],
            recv_sem=recv.at[slot],
            device_id=partner,
            device_id_type=MESH,
        ).wait_recv()

    def send_own(args):
        @pl.when(has_up)
        def _():
            line(*args, z, 0).start()

        @pl.when(has_down)
        def _():
            line(*args, z, 1).start()

        line(*args, z, 2).start()

    def relay(args, s):
        @pl.when(z - s >= 0)
        def _():
            arrived(*args, (z - s) * 2 + core)

            @pl.when(has_up)
            def _():
                line(*args, z - s, 0).start()

            line(*args, z - s, 2).start()

        @pl.when(z + s <= n_z - 1)
        def _():
            arrived(*args, (z + s) * 2 + core)

            @pl.when(has_down)
            def _():
                line(*args, z + s, 1).start()

            line(*args, z + s, 2).start()

    def drain(args):
        def step(origin, carry):
            @pl.when(jnp.logical_and(origin <= z, has_up))
            def _():
                line(*args, origin, 0).wait_send()

            @pl.when(jnp.logical_and(origin >= z, has_down))
            def _():
                line(*args, origin, 1).wait_send()

            line(*args, origin, 2).wait_send()
            return carry

        lax.fori_loop(0, n_z, step, 0)

    xd_args = (xd, xd_send, xd_recv)
    nb_args = (nb, nb_send, nb_recv)

    own_xd = pltpu.make_async_copy(xd_in, xd.at[mp], own_sem.at[0])
    own_rows = pltpu.make_async_copy(
        rows_in.at[dp], nb.at[mp, pl.ds(dp * block, block)], own_sem.at[1]
    )
    own_tags = pltpu.make_async_copy(tags_in.at[dp], tags.at[dp], own_sem.at[2])
    own_xd.start()
    own_rows.start()
    own_tags.start()
    greet(
        [(None, {"dp": peer(k)}) for k in range(1, n_dp)]
        + [(None, partner), (has_up, up), (has_down, down)]
    )

    def row_copy(k):
        to = peer(k)
        return pltpu.make_async_remote_copy(
            src_ref=rows_in.at[to],
            dst_ref=nb.at[mp, pl.ds(dp * block, block)],
            send_sem=a2a_send.at[k],
            recv_sem=a2a_recv.at[k],
            device_id={"dp": to},
            device_id_type=MESH,
        )

    def tag_copy(k):
        to = peer(k)
        return pltpu.make_async_remote_copy(
            src_ref=tags_in.at[to],
            dst_ref=tags.at[dp],
            send_sem=tag_send.at[k],
            recv_sem=tag_recv.at[k],
            device_id={"dp": to},
            device_id_type=MESH,
        )

    for k in range(1, n_dp):
        row_copy(k).start()
    for k in range(1, n_dp):
        tag_copy(k).start()
    own_xd.wait()
    send_own(xd_args)
    for copy in weight_copies:
        copy.start()
    own_rows.wait()
    for k in range(1, n_dp):
        row_copy(k).wait()
    send_own(nb_args)
    own_tags.wait()
    for k in range(1, n_dp):
        tag_copy(k).wait()

    def xd_step(s, carry):
        relay(xd_args, s)
        return carry

    lax.fori_loop(1, n_z, xd_step, 0)

    span_len = tokens // (counts_in.shape[0])
    lane = lax.broadcasted_iota(jnp.int32, (1, tokens), 1)
    spans = counts_in.shape[0]
    first = jnp.zeros((1, tokens), jnp.int32)
    limit = jnp.zeros((1, tokens), jnp.int32)
    for c in range(spans):
        here = jnp.logical_and(lane >= c * span_len, lane < (c + 1) * span_len)
        first = jnp.where(here, (dp * spans + c) * MAXN, first)
        limit = jnp.where(here, counts_in[c : c + 1, :], limit)
    width = block // capacity
    for g in range(n_dp):
        for i in range(capacity):
            tag = tags[g, i : i + 1, :]
            place = tag - first
            live = jnp.logical_and(tag >= 0, jnp.logical_and(place >= 0, place < limit))
            value = jnp.where(live, 0.0, -jnp.inf)
            low = (g * capacity + i) * width
            bias[low : low + width, :] = jnp.broadcast_to(value, (width, tokens))

    scale = 1.0 / math.sqrt(DH)

    def project(slot):
        rows = nb[slot]
        k_rows = dot_f32(rows, wk[...]).astype(jnp.bfloat16)
        v_rows = dot_f32(rows, wv[...]).astype(jnp.bfloat16)
        vals[slot] = v_rows
        for h in range(queries.shape[1] // DH):
            cols = slice(h * DH, (h + 1) * DH)
            scores[h, slot] = dot_f32(k_rows[:, cols], queries[:, cols], NT) * scale + bias[...]
            grad_w[h, slot] = dot_f32(v_rows[:, cols], grads[:, cols], NT)

    def both_cores(origin):
        arrived(*nb_args, origin * 2 + 1 - core)

        def step(c, carry):
            project(origin * 2 + c)
            return carry

        lax.fori_loop(0, 2, step, 0)

    def nb_step(s, carry):
        relay(nb_args, s)

        @pl.when(s == 1)
        def _():
            for copy in weight_copies:
                copy.wait()

            def other(origin, c):
                arrived(*xd_args, origin * 2 + 1 - core)
                return c

            lax.fori_loop(0, n_z, other, 0)

            def add(m, c):
                q, g = c
                cols = pl.ds(pl.multiple_of(m * feat, feat), feat)
                q = q + dot_f32(xd[m, :tokens, :], wq[cols, :])
                g = g + dot_f32(xd[m, tokens:, :], wo[:, cols], NT)
                return (q, g)

            zero = jnp.zeros(queries.shape, jnp.float32)
            q, g = lax.fori_loop(0, n_mp, add, (zero, zero))
            queries[...] = q.astype(jnp.bfloat16)
            grads[...] = g.astype(jnp.bfloat16)
            both_cores(z)

        @pl.when(z - s >= 0)
        def _():
            both_cores(z - s)

        @pl.when(z + s <= n_z - 1)
        def _():
            both_cores(z + s)

        return carry

    lax.fori_loop(1, n_z, nb_step, 0)

    shard = nb.shape[1]
    total = n_mp * shard
    for h in range(queries.shape[1] // DH):
        cols = slice(h * DH, (h + 1) * DH)
        q = queries[:, cols]
        g = grads[:, cols]
        v = vals[:, :, cols].reshape(total, DH)
        score = scores[h].reshape(total, tokens)
        peak = jnp.max(score, axis=0, keepdims=True)
        expo = jnp.exp(score - peak)
        weights = expo * (1.0 / jnp.sum(expo, axis=0, keepdims=True))
        weights_bf = weights.astype(jnp.bfloat16)
        att_out[:, cols] = dot_f32(weights_bf, v, TN).astype(jnp.bfloat16)
        gv_out[:, :, cols] = dot_f32(weights_bf, g).astype(jnp.bfloat16).reshape(n_mp, shard, DH)
        grad_h = grad_w[h].reshape(total, tokens)
        inner = jnp.sum(weights * grad_h, axis=0, keepdims=True)
        grad_s = (weights * (grad_h - inner) * scale).astype(jnp.bfloat16)
        gk_out[:, :, cols] = dot_f32(grad_s, q).astype(jnp.bfloat16).reshape(n_mp, shard, DH)

    drain(xd_args)
    drain(nb_args)


def forward(xd_shard, send_rows, send_tags, counts_rows, w_query, w_key, w_value, w_out, n_dp, n_mp):
    capacity = send_tags.shape[1]
    tokens = xd_shard.shape[0] // 2
    send_tags = jnp.broadcast_to(
        jnp.pad(send_tags, ((0, 0), (0, -capacity % 8)), constant_values=-1)[:, :, None],
        (n_dp, capacity + (-capacity % 8), tokens),
    )
    shard = n_dp * send_rows.shape[1]
    enc = send_rows.shape[2]
    width = w_query.shape[1]

    bf = jnp.bfloat16
    n_z = n_mp // 2
    hbm = pl.BlockSpec(memory_space=pl.ANY)
    vm = pl.BlockSpec(memory_space=pltpu.VMEM)
    dma = pltpu.SemaphoreType.DMA
    return pl.pallas_call(
        functools.partial(forward_kernel, n_dp, n_mp, capacity),
        out_shape=(
            jax.ShapeDtypeStruct((tokens, width), bf),
            jax.ShapeDtypeStruct((n_mp, shard, width), bf),
            jax.ShapeDtypeStruct((n_mp, shard, width), bf),
        ),
        in_specs=[hbm, hbm, hbm, vm, hbm, hbm, hbm, hbm],
        out_specs=(vm, vm, vm),
        scratch_shapes=[
            pltpu.VMEM((n_mp,) + xd_shard.shape, bf),
            pltpu.VMEM((n_mp, shard, enc), bf),
            pltpu.VMEM(send_tags.shape, jnp.int32),
            pltpu.VMEM(w_query.shape, bf),
            pltpu.VMEM(w_key.shape, bf),
            pltpu.VMEM(w_value.shape, bf),
            pltpu.VMEM(w_out.shape, bf),
            pltpu.VMEM((width // DH, n_mp, shard, tokens), jnp.float32),
            pltpu.VMEM((width // DH, n_mp, shard, tokens), jnp.float32),
            pltpu.VMEM((n_mp, shard, width), bf),
            pltpu.VMEM((tokens, width), bf),
            pltpu.VMEM((tokens, width), bf),
            pltpu.VMEM((shard, tokens), jnp.float32),
            dma((4,)),
            dma((n_dp,)),
            dma((n_dp,)),
            dma((n_dp,)),
            dma((n_dp,)),
            dma((3,)),
            dma((3, n_z)),
            dma((n_mp,)),
            dma((3, n_z)),
            dma((n_mp,)),
        ],
        compiler_params=pltpu.CompilerParams(
            collective_id=0, has_side_effects=True, vmem_limit_bytes=VMEM_LIMIT
        ),
        name="gather_attend",
    )(xd_shard, send_rows, send_tags, counts_rows, w_query, w_key, w_value, w_out)


def backward_kernel(
    n_dp,
    n_mp,
    att,
    gk,
    gv,
    wk_in,
    wv_in,
    wo_in,
    layer_out,
    returned,
    wk,
    wv,
    wo,
    mine,
    theirs,
    paired,
    landed,
    out_mine,
    out_theirs,
    out_paired,
    out_landed,
    w_sem,
    pair_send,
    pair_recv,
    out_pair_send,
    out_pair_recv,
    hop_send,
    hop_recv,
    out_send,
    out_recv,
    a2a_send,
    a2a_recv,
    own_sem,
):
    dp = lax.axis_index("dp")
    mp = lax.axis_index("mp")
    n_z = n_mp // 2
    z = mp // 2
    core = mp % 2
    partner = {"mp": mp + 1 - 2 * core}
    up = {"mp": lax.rem(mp + 2, n_mp)}
    down = {"mp": lax.rem(mp + n_mp - 2, n_mp)}
    has_up = z < n_z - 1
    has_down = z > 0
    chunk = mine.shape[1] // n_dp
    feat = out_mine.shape[2]
    bf = jnp.bfloat16

    weight_copies = [
        pltpu.make_async_copy(src, dst, w_sem.at[i])
        for i, (src, dst) in enumerate(((wk_in, wk), (wv_in, wv), (wo_in, wo)))
    ]
    for copy in weight_copies:
        copy.start()
    greet(
        [(None, {"dp": lax.rem(dp + k, n_dp)}) for k in range(1, n_dp)]
        + [(None, partner), (has_up, up), (has_down, down)]
    )
    for copy in weight_copies:
        copy.wait()

    def pair_copy(d):
        return pltpu.make_async_remote_copy(
            src_ref=theirs.at[d],
            dst_ref=paired.at[d],
            send_sem=pair_send.at[d],
            recv_sem=pair_recv.at[d],
            device_id=partner,
            device_id_type=MESH,
        )

    def out_pair_copy(d):
        return pltpu.make_async_remote_copy(
            src_ref=out_theirs.at[d],
            dst_ref=out_paired.at[d],
            send_sem=out_pair_send.at[d],
            recv_sem=out_pair_recv.at[d],
            device_id=partner,
            device_id_type=MESH,
        )

    def grad_part(m):
        return (dot_f32(gk[m], wk[...], NT) + dot_f32(gv[m], wv[...], NT)).astype(bf)

    def out_part(m):
        cols = pl.ds(pl.multiple_of(m * feat, feat), feat)
        return dot_f32(att[...], wo[:, cols]).astype(bf)

    def add(a, b):
        return (a.astype(jnp.float32) + b.astype(jnp.float32)).astype(bf)

    def start_parts(d):
        own, other = d * 2 + core, d * 2 + 1 - core
        theirs[d] = grad_part(other)
        pair_copy(d).start()
        out_theirs[d] = out_part(other)
        out_pair_copy(d).start()
        mine[d] = grad_part(own)
        out_mine[d] = out_part(own)

    def finish_parts(d):
        out_pair_copy(d).wait()
        out_mine[d] = add(out_mine[d], out_paired[d])
        pair_copy(d).wait()
        mine[d] = add(mine[d], paired[d])

    def target(direction, k):
        j = k // n_dp
        return n_z - 1 - j if direction == 0 else j

    def slot_of(direction, d):
        return d if direction == 0 else jnp.where(d == z - 1, n_z, d)

    def hop(direction, k):
        d = target(direction, k)
        rows = pl.ds(pl.multiple_of((k % n_dp) * chunk, chunk), chunk)
        slot = slot_of(direction, d)
        return pltpu.make_async_remote_copy(
            src_ref=mine.at[d, rows],
            dst_ref=landed.at[slot, rows],
            send_sem=hop_send.at[direction, k],
            recv_sem=hop_recv.at[slot, k % n_dp],
            device_id=(up, down)[direction],
            device_id_type=MESH,
        )

    def hop_arrived(slot, g):
        rows = pl.ds(pl.multiple_of(g * chunk, chunk), chunk)
        pltpu.make_async_remote_copy(
            src_ref=landed.at[slot, rows],
            dst_ref=landed.at[slot, rows],
            send_sem=hop_send.at[0, 0],
            recv_sem=hop_recv.at[slot, g],
            device_id=partner,
            device_id_type=MESH,
        ).wait_recv()
        return rows

    def out_hop(direction, j):
        d = n_z - 1 - j if direction == 0 else j
        slot = slot_of(direction, d)
        return pltpu.make_async_remote_copy(
            src_ref=out_mine.at[d],
            dst_ref=out_landed.at[slot],
            send_sem=out_send.at[direction, j],
            recv_sem=out_recv.at[slot],
            device_id=(up, down)[direction],
            device_id_type=MESH,
        )

    def out_arrived(slot):
        pltpu.make_async_remote_copy(
            src_ref=out_landed.at[slot],
            dst_ref=out_landed.at[slot],
            send_sem=out_send.at[0, 0],
            recv_sem=out_recv.at[slot],
            device_id=partner,
            device_id_type=MESH,
        ).wait_recv()

    sent = (n_z - 1 - z, z)
    from_behind = (has_down, has_up)

    def at_step(s):
        items = []
        for direction in range(2):
            j = s - (z if direction == 0 else n_z - 1 - z)
            d = n_z - 1 - j if direction == 0 else j
            items.append((direction, j, d, jnp.logical_and(j >= 0, j < sent[direction])))
        return items

    @pl.when(jnp.logical_or(z == 0, z == n_z - 1))
    def _():
        start_parts(n_z - 1 - z)

    def step(s, carry):
        items = at_step(s)
        following = at_step(s + 1)
        for direction, j, d, active in items:

            @pl.when(active)
            def _(d=d):
                finish_parts(d)

        for direction, j, d, active in items:

            @pl.when(active)
            def _(direction=direction, j=j, d=d):
                @pl.when(from_behind[direction])
                def _():
                    out_arrived(d)
                    out_mine[d] = add(out_mine[d], out_landed[d])

                out_hop(direction, j).start()

        def each(g, c):
            for direction, j, d, active in items:

                @pl.when(active)
                def _(direction=direction, j=j, d=d):
                    @pl.when(from_behind[direction])
                    def _():
                        rows = hop_arrived(d, g)
                        mine[d, rows, :] = add(mine[d, rows, :], landed[d, rows, :])

                    k = j * n_dp + g

                    @pl.when(k >= 2)
                    def _():
                        hop(direction, k - 2).wait_send()

                    hop(direction, k).start()

            wanted = jnp.logical_and(g == 2, s == n_z - 2)
            part = z
            for direction, j, d, active in following:
                here = g == direction
                wanted = jnp.logical_or(wanted, jnp.logical_and(here, active))
                part = jnp.where(here, d, part)

            @pl.when(wanted)
            def _():
                start_parts(part)

            return c

        lax.fori_loop(0, n_dp, each, 0)
        return carry

    lax.fori_loop(0, n_z - 1, step, 0)

    finish_parts(z)

    @pl.when(has_down)
    def _():
        out_arrived(z)
        out_mine[z] = add(out_mine[z], out_landed[z])

    @pl.when(has_up)
    def _():
        out_arrived(n_z)
        out_mine[z] = add(out_mine[z], out_landed[n_z])

    layer_out[...] = out_mine[z]

    def back(g):
        rows = pl.ds(pl.multiple_of(g * chunk, chunk), chunk)
        return pltpu.make_async_remote_copy(
            src_ref=mine.at[z, rows],
            dst_ref=returned.at[dp],
            send_sem=a2a_send.at[g],
            recv_sem=a2a_recv.at[dp],
            device_id={"dp": g},
            device_id_type=MESH,
        )

    def back_arrived(g):
        rows = pl.ds(pl.multiple_of(g * chunk, chunk), chunk)
        pltpu.make_async_remote_copy(
            src_ref=mine.at[z, rows],
            dst_ref=returned.at[g],
            send_sem=a2a_send.at[g],
            recv_sem=a2a_recv.at[g],
            device_id={"dp": g},
            device_id_type=MESH,
        ).wait_recv()

    own_rows = pl.ds(pl.multiple_of(dp * chunk, chunk), chunk)
    own_copy = pltpu.make_async_copy(mine.at[z, own_rows], returned.at[dp], own_sem)

    def last(g, c):
        rows = pl.ds(pl.multiple_of(g * chunk, chunk), chunk)

        @pl.when(has_down)
        def _():
            hop_arrived(z, g)
            mine[z, rows, :] = add(mine[z, rows, :], landed[z, rows, :])

        @pl.when(has_up)
        def _():
            hop_arrived(n_z, g)
            mine[z, rows, :] = add(mine[z, rows, :], landed[n_z, rows, :])

        @pl.when(g != dp)
        def _():
            back(g).start()

        @pl.when(g == dp)
        def _():
            own_copy.start()

        return c

    lax.fori_loop(0, n_dp, last, 0)
    own_copy.wait()

    def finish(g, c):
        @pl.when(g != dp)
        def _():
            back(g).wait_send()
            back_arrived(g)

        return c

    lax.fori_loop(0, n_dp, finish, 0)

    for direction in range(2):

        @pl.when(sent[direction] > 0)
        def _(direction=direction):
            count = sent[direction] * n_dp
            hop(direction, count - 2).wait_send()
            hop(direction, count - 1).wait_send()

        def drain(j, c, direction=direction):
            @pl.when(j < sent[direction])
            def _():
                out_hop(direction, j).wait_send()

            return c

        lax.fori_loop(0, n_z - 1, drain, 0)


def backward(att, gk, gv, w_key, w_value, w_out, n_dp, n_mp):
    tokens = att.shape[0]
    shard = gk.shape[1]
    enc = w_key.shape[0]
    feat = w_out.shape[1] // n_mp
    n_z = n_mp // 2
    bf = jnp.bfloat16
    hbm = pl.BlockSpec(memory_space=pl.ANY)
    vm = pl.BlockSpec(memory_space=pltpu.VMEM)
    dma = pltpu.SemaphoreType.DMA
    return pl.pallas_call(
        functools.partial(backward_kernel, n_dp, n_mp),
        out_shape=(
            jax.ShapeDtypeStruct((tokens, feat), bf),
            jax.ShapeDtypeStruct((n_dp, shard // n_dp, enc), bf),
        ),
        in_specs=[vm, vm, vm, hbm, hbm, hbm],
        out_specs=(vm, hbm),
        scratch_shapes=[
            pltpu.VMEM(w_key.shape, bf),
            pltpu.VMEM(w_value.shape, bf),
            pltpu.VMEM(w_out.shape, bf),
            pltpu.VMEM((n_z, shard, enc), bf),
            pltpu.VMEM((n_z, shard, enc), bf),
            pltpu.VMEM((n_z, shard, enc), bf),
            pltpu.VMEM((n_z + 1, shard, enc), bf),
            pltpu.VMEM((n_z, tokens, feat), bf),
            pltpu.VMEM((n_z, tokens, feat), bf),
            pltpu.VMEM((n_z, tokens, feat), bf),
            pltpu.VMEM((n_z + 1, tokens, feat), bf),
            dma((3,)),
            dma((n_z,)),
            dma((n_z,)),
            dma((n_z,)),
            dma((n_z,)),
            dma((2, n_z * n_dp)),
            dma((n_z + 1, n_dp)),
            dma((2, n_z)),
            dma((n_z + 1,)),
            dma((n_dp,)),
            dma((n_dp,)),
            dma,
        ],
        compiler_params=pltpu.CompilerParams(
            collective_id=1, has_side_effects=True, vmem_limit_bytes=VMEM_LIMIT
        ),
        name="grads_scatter",
    )(att, gk, gv, w_key, w_value, w_out)


def per_device(hidden_in, out_grad, neighbours, counts, slot_owner, w_query, w_key, w_value, w_out):
    groups = lax.axis_size("dp")
    n_mp = lax.axis_size("mp")
    spans = counts.shape[0]
    slots_group = spans * MAXN
    src_slots = slot_owner.shape[0]
    capacity = src_slots // groups
    rows_dev = neighbours.shape[1]
    enc_width = neighbours.shape[2]
    slot_order = jnp.arange(src_slots, dtype=jnp.int32)
    dest_group = jnp.where(slot_owner >= 0, slot_owner // slots_group, -1)
    earlier = (dest_group[None, :] == dest_group[:, None]) & (
        slot_order[None, :] < slot_order[:, None]
    )
    rank_in = jnp.sum(earlier.astype(jnp.int32), axis=1)
    position = jnp.where(slot_owner >= 0, dest_group * capacity + rank_in, -1)
    picked = position[None, :] == slot_order[:, None]
    source = jnp.sum(jnp.where(picked, slot_order[None, :], 0), axis=1)
    filled = jnp.any(picked, axis=1)
    send_rows = jnp.where(
        filled[:, None, None], jnp.take(neighbours, source, axis=0), jnp.zeros((), jnp.bfloat16)
    )
    send_rows = send_rows.reshape(groups, capacity * rows_dev, enc_width)
    send_tags = jnp.sum(
        jnp.where(picked, slot_owner[None, :] + 1, 0), axis=1
    ).reshape(groups, capacity) - 1
    counts_rows = jnp.broadcast_to(counts[:, None], (spans, hidden_in.shape[0]))
    attended, grad_keys, grad_values = forward(
        jnp.concatenate([hidden_in, out_grad], axis=0),
        send_rows,
        send_tags,
        counts_rows,
        w_query,
        w_key,
        w_value,
        w_out,
        groups,
        n_mp,
    )
    layer_out, returned = backward(
        attended, grad_keys, grad_values, w_key, w_value, w_out, groups, n_mp
    )
    returned = returned.reshape(src_slots, rows_dev, enc_width)
    neighbour_grad = jnp.where(
        (slot_owner >= 0)[:, None, None],
        jnp.take(returned, jnp.maximum(position, 0), axis=0),
        jnp.zeros((), jnp.bfloat16),
    )
    return (layer_out, neighbour_grad)


def solution(mesh):
    return jax.shard_map(
        per_device,
        mesh=mesh,
        in_specs=(
            P("dp", "mp"),
            P("dp", "mp"),
            P("dp", "mp", None),
            P("dp"),
            P("dp"),
            P(None, "mp"),
            P(None, "mp"),
            P(None, "mp"),
            P("mp", None),
        ),
        out_specs=(P("dp", "mp"), P("dp", "mp", None)),
        check_vma=False,
    )
```

```python
import functools
import math

import jax
import jax.numpy as jnp
from jax import lax
from jax.experimental import pallas as pl
from jax.experimental.pallas import tpu as pltpu
from jax.sharding import PartitionSpec as P

DH = 128
MAXN = 10
MESH = pl.DeviceIdType.MESH
NT = (((1,), (1,)), ((), ()))
TN = (((0,), (0,)), ((), ()))
VMEM_LIMIT = 62 * 1024 * 1024


def dot_f32(a, b, dims=(((1,), (0,)), ((), ()))):
    return lax.dot_general(a, b, dims, preferred_element_type=jnp.float32)


def greet(peers):
    barrier = pltpu.get_barrier_semaphore()
    total = 0
    for cond, dev in peers:
        if cond is None:
            pl.semaphore_signal(barrier, inc=1, device_id=dev, device_id_type=MESH)
            total = total + 1
        else:

            @pl.when(cond)
            def _(dev=dev):
                pl.semaphore_signal(barrier, inc=1, device_id=dev, device_id_type=MESH)

            total = total + jnp.where(cond, 1, 0)
    pl.semaphore_wait(barrier, total)


def forward_kernel(
    n_dp,
    n_mp,
    capacity,
    x_in,
    dy_in,
    rows_in,
    tags_in,
    counts_in,
    wq_in,
    wk_in,
    wv_in,
    wo_in,
    att_out,
    gk_out,
    gv_out,
    xd,
    nb,
    tags,
    wq,
    wk,
    wv,
    wo,
    scores,
    grad_w,
    vals,
    queries,
    grads,
    bias,
    w_sem,
    a2a_send,
    a2a_recv,
    tag_send,
    tag_recv,
    own_sem,
    xd_send,
    xd_recv,
    nb_send,
    nb_recv,
):
    dp = lax.axis_index("dp")
    mp = lax.axis_index("mp")
    n_z = n_mp // 2
    z = mp // 2
    core = mp % 2
    partner = {"mp": mp + 1 - 2 * core}
    up = {"mp": lax.rem(mp + 2, n_mp)}
    down = {"mp": lax.rem(mp + n_mp - 2, n_mp)}
    has_up = z < n_z - 1
    has_down = z > 0
    block = nb.shape[1] // n_dp
    tokens = att_out.shape[0]
    feat = xd.shape[2]

    def peer(k):
        return lax.rem(dp + k, n_dp)

    weight_copies = [
        pltpu.make_async_copy(src, dst, w_sem.at[i])
        for i, (src, dst) in enumerate(((wq_in, wq), (wo_in, wo), (wk_in, wk), (wv_in, wv)))
    ]

    def line(buf, send, recv, origin, direction):
        slot = origin * 2 + core
        return pltpu.make_async_remote_copy(
            src_ref=buf.at[slot],
            dst_ref=buf.at[slot],
            send_sem=send.at[direction, origin],
            recv_sem=recv.at[slot],
            device_id=(up, down, partner)[direction],
            device_id_type=MESH,
        )

    def arrived(buf, send, recv, slot):
        pltpu.make_async_remote_copy(
            src_ref=buf.at[slot],
            dst_ref=buf.at[slot],
            send_sem=send.at[0, 0],
            recv_sem=recv.at[slot],
            device_id=partner,
            device_id_type=MESH,
        ).wait_recv()

    def send_own(args):
        @pl.when(has_up)
        def _():
            line(*args, z, 0).start()

        @pl.when(has_down)
        def _():
            line(*args, z, 1).start()

        line(*args, z, 2).start()

    def relay(args, s):
        @pl.when(z - s >= 0)
        def _():
            arrived(*args, (z - s) * 2 + core)

            @pl.when(has_up)
            def _():
                line(*args, z - s, 0).start()

            line(*args, z - s, 2).start()

        @pl.when(z + s <= n_z - 1)
        def _():
            arrived(*args, (z + s) * 2 + core)

            @pl.when(has_down)
            def _():
                line(*args, z + s, 1).start()

            line(*args, z + s, 2).start()

    def drain(args):
        def step(origin, carry):
            @pl.when(jnp.logical_and(origin <= z, has_up))
            def _():
                line(*args, origin, 0).wait_send()

            @pl.when(jnp.logical_and(origin >= z, has_down))
            def _():
                line(*args, origin, 1).wait_send()

            line(*args, origin, 2).wait_send()
            return carry

        lax.fori_loop(0, n_z, step, 0)

    xd_args = (xd, xd_send, xd_recv)
    nb_args = (nb, nb_send, nb_recv)

    own_x = pltpu.make_async_copy(x_in, xd.at[mp, pl.ds(0, tokens)], own_sem.at[0])
    own_dy = pltpu.make_async_copy(dy_in, xd.at[mp, pl.ds(tokens, tokens)], own_sem.at[3])
    own_rows = pltpu.make_async_copy(
        rows_in.at[dp], nb.at[mp, pl.ds(dp * block, block)], own_sem.at[1]
    )
    own_tags = pltpu.make_async_copy(tags_in.at[dp], tags.at[dp], own_sem.at[2])
    own_x.start()
    own_dy.start()
    own_rows.start()
    own_tags.start()
    greet(
        [(None, {"dp": peer(k)}) for k in range(1, n_dp)]
        + [(None, partner), (has_up, up), (has_down, down)]
    )

    def row_copy(k):
        to = peer(k)
        return pltpu.make_async_remote_copy(
            src_ref=rows_in.at[to],
            dst_ref=nb.at[mp, pl.ds(dp * block, block)],
            send_sem=a2a_send.at[k],
            recv_sem=a2a_recv.at[k],
            device_id={"dp": to},
            device_id_type=MESH,
        )

    def tag_copy(k):
        to = peer(k)
        return pltpu.make_async_remote_copy(
            src_ref=tags_in.at[to],
            dst_ref=tags.at[dp],
            send_sem=tag_send.at[k],
            recv_sem=tag_recv.at[k],
            device_id={"dp": to},
            device_id_type=MESH,
        )

    for k in range(1, n_dp):
        row_copy(k).start()
    for k in range(1, n_dp):
        tag_copy(k).start()
    own_x.wait()
    own_dy.wait()
    send_own(xd_args)
    for copy in weight_copies:
        copy.start()
    own_rows.wait()
    for k in range(1, n_dp):
        row_copy(k).wait()
    send_own(nb_args)
    own_tags.wait()
    for k in range(1, n_dp):
        tag_copy(k).wait()

    def xd_step(s, carry):
        relay(xd_args, s)
        return carry

    lax.fori_loop(1, n_z, xd_step, 0)

    span_len = tokens // (counts_in.shape[0])
    lane = lax.broadcasted_iota(jnp.int32, (1, tokens), 1)
    spans = counts_in.shape[0]
    first = jnp.zeros((1, tokens), jnp.int32)
    limit = jnp.zeros((1, tokens), jnp.int32)
    for c in range(spans):
        here = jnp.logical_and(lane >= c * span_len, lane < (c + 1) * span_len)
        first = jnp.where(here, (dp * spans + c) * MAXN, first)
        limit = jnp.where(here, counts_in[c : c + 1, :], limit)
    width = block // capacity
    for g in range(n_dp):
        for i in range(capacity):
            tag = tags[g, i : i + 1, :]
            place = tag - first
            live = jnp.logical_and(tag >= 0, jnp.logical_and(place >= 0, place < limit))
            value = jnp.where(live, 0.0, -jnp.inf)
            low = (g * capacity + i) * width
            bias[low : low + width, :] = jnp.broadcast_to(value, (width, tokens))

    scale = 1.0 / math.sqrt(DH)

    def project(slot):
        rows = nb[slot]
        k_rows = dot_f32(rows, wk[...]).astype(jnp.bfloat16)
        v_rows = dot_f32(rows, wv[...]).astype(jnp.bfloat16)
        vals[slot] = v_rows
        for h in range(queries.shape[1] // DH):
            cols = slice(h * DH, (h + 1) * DH)
            scores[h, slot] = dot_f32(k_rows[:, cols], queries[:, cols], NT) * scale + bias[...]
            grad_w[h, slot] = dot_f32(v_rows[:, cols], grads[:, cols], NT)

    def both_cores(origin):
        def step(i, carry):
            slot = origin * 2 + jnp.where(i == 0, core, 1 - core)

            @pl.when(i == 1)
            def _():
                arrived(*nb_args, slot)

            project(slot)
            return carry

        lax.fori_loop(0, 2, step, 0)

    def nb_step(s, carry):
        relay(nb_args, s)

        @pl.when(s == 1)
        def _():
            for copy in weight_copies:
                copy.wait()

            def other(origin, c):
                arrived(*xd_args, origin * 2 + 1 - core)
                return c

            lax.fori_loop(0, n_z, other, 0)

            def add(m, c):
                q, g = c
                cols = pl.ds(pl.multiple_of(m * feat, feat), feat)
                q = q + dot_f32(xd[m, :tokens, :], wq[cols, :])
                g = g + dot_f32(xd[m, tokens:, :], wo[:, cols], NT)
                return (q, g)

            zero = jnp.zeros(queries.shape, jnp.float32)
            q, g = lax.fori_loop(0, n_mp, add, (zero, zero))
            queries[...] = q.astype(jnp.bfloat16)
            grads[...] = g.astype(jnp.bfloat16)
            both_cores(z)

        @pl.when(z - s >= 0)
        def _():
            both_cores(z - s)

        @pl.when(z + s <= n_z - 1)
        def _():
            both_cores(z + s)

        return carry

    lax.fori_loop(1, n_z, nb_step, 0)

    shard = nb.shape[1]
    total = n_mp * shard
    for h in range(queries.shape[1] // DH):
        cols = slice(h * DH, (h + 1) * DH)
        q = queries[:, cols]
        g = grads[:, cols]
        v = vals[:, :, cols].reshape(total, DH)
        score = scores[h].reshape(total, tokens)
        peak = jnp.max(score, axis=0, keepdims=True)
        expo = jnp.exp(score - peak)
        weights = expo * (1.0 / jnp.sum(expo, axis=0, keepdims=True))
        weights_bf = weights.astype(jnp.bfloat16)
        att_out[:, cols] = dot_f32(weights_bf, v, TN).astype(jnp.bfloat16)
        gv_out[:, :, cols] = dot_f32(weights_bf, g).astype(jnp.bfloat16).reshape(n_mp, shard, DH)
        grad_h = grad_w[h].reshape(total, tokens)
        inner = jnp.sum(weights * grad_h, axis=0, keepdims=True)
        grad_s = (weights * (grad_h - inner) * scale).astype(jnp.bfloat16)
        gk_out[:, :, cols] = dot_f32(grad_s, q).astype(jnp.bfloat16).reshape(n_mp, shard, DH)

    drain(xd_args)
    drain(nb_args)


def forward(x_shard, dy_shard, send_rows, send_tags, counts_rows, w_query, w_key, w_value, w_out, n_dp, n_mp):
    capacity = send_tags.shape[1]
    tokens, feat = x_shard.shape
    send_tags = jnp.broadcast_to(
        jnp.pad(send_tags, ((0, 0), (0, -capacity % 8)), constant_values=-1)[:, :, None],
        (n_dp, capacity + (-capacity % 8), tokens),
    )
    shard = n_dp * send_rows.shape[1]
    enc = send_rows.shape[2]
    width = w_query.shape[1]

    bf = jnp.bfloat16
    n_z = n_mp // 2
    hbm = pl.BlockSpec(memory_space=pl.ANY)
    vm = pl.BlockSpec(memory_space=pltpu.VMEM)
    dma = pltpu.SemaphoreType.DMA
    return pl.pallas_call(
        functools.partial(forward_kernel, n_dp, n_mp, capacity),
        out_shape=(
            jax.ShapeDtypeStruct((tokens, width), bf),
            jax.ShapeDtypeStruct((n_mp, shard, width), bf),
            jax.ShapeDtypeStruct((n_mp, shard, width), bf),
        ),
        in_specs=[hbm, hbm, hbm, hbm, vm, hbm, hbm, hbm, hbm],
        out_specs=(vm, vm, vm),
        scratch_shapes=[
            pltpu.VMEM((n_mp, 2 * tokens, feat), bf),
            pltpu.VMEM((n_mp, shard, enc), bf),
            pltpu.VMEM(send_tags.shape, jnp.int32),
            pltpu.VMEM(w_query.shape, bf),
            pltpu.VMEM(w_key.shape, bf),
            pltpu.VMEM(w_value.shape, bf),
            pltpu.VMEM(w_out.shape, bf),
            pltpu.VMEM((width // DH, n_mp, shard, tokens), jnp.float32),
            pltpu.VMEM((width // DH, n_mp, shard, tokens), jnp.float32),
            pltpu.VMEM((n_mp, shard, width), bf),
            pltpu.VMEM((tokens, width), bf),
            pltpu.VMEM((tokens, width), bf),
            pltpu.VMEM((shard, tokens), jnp.float32),
            dma((4,)),
            dma((n_dp,)),
            dma((n_dp,)),
            dma((n_dp,)),
            dma((n_dp,)),
            dma((4,)),
            dma((3, n_z)),
            dma((n_mp,)),
            dma((3, n_z)),
            dma((n_mp,)),
        ],
        compiler_params=pltpu.CompilerParams(
            collective_id=0, has_side_effects=True, vmem_limit_bytes=VMEM_LIMIT
        ),
        name="gather_attend",
    )(x_shard, dy_shard, send_rows, send_tags, counts_rows, w_query, w_key, w_value, w_out)


def backward_kernel(
    n_dp,
    n_mp,
    att,
    gk_in,
    gv_in,
    wk_in,
    wv_in,
    wo_in,
    layer_out,
    returned,
    gk,
    gv,
    wk,
    wv,
    wo,
    mine,
    theirs,
    paired,
    landed,
    out_mine,
    out_theirs,
    out_paired,
    out_landed,
    w_sem,
    pair_send,
    pair_recv,
    out_pair_send,
    out_pair_recv,
    hop_send,
    hop_recv,
    out_send,
    out_recv,
    a2a_send,
    a2a_recv,
    own_sem,
):
    dp = lax.axis_index("dp")
    mp = lax.axis_index("mp")
    n_z = n_mp // 2
    z = mp // 2
    core = mp % 2
    partner = {"mp": mp + 1 - 2 * core}
    up = {"mp": lax.rem(mp + 2, n_mp)}
    down = {"mp": lax.rem(mp + n_mp - 2, n_mp)}
    has_up = z < n_z - 1
    has_down = z > 0
    chunk = mine.shape[1] // n_dp
    feat = out_mine.shape[2]
    bf = jnp.bfloat16

    weight_copies = [
        pltpu.make_async_copy(src, dst, w_sem.at[i])
        for i, (src, dst) in enumerate(
            ((wk_in, wk), (wv_in, wv), (gk_in, gk), (gv_in, gv), (wo_in, wo))
        )
    ]
    for copy in weight_copies:
        copy.start()
    greet(
        [(None, {"dp": lax.rem(dp + k, n_dp)}) for k in range(1, n_dp)]
        + [(None, partner), (has_up, up), (has_down, down)]
    )
    for copy in weight_copies[:-1]:
        copy.wait()

    def pair_copy(d):
        return pltpu.make_async_remote_copy(
            src_ref=theirs.at[d],
            dst_ref=paired.at[d],
            send_sem=pair_send.at[d],
            recv_sem=pair_recv.at[d],
            device_id=partner,
            device_id_type=MESH,
        )

    def out_pair_copy(d):
        return pltpu.make_async_remote_copy(
            src_ref=out_theirs.at[d],
            dst_ref=out_paired.at[d],
            send_sem=out_pair_send.at[d],
            recv_sem=out_pair_recv.at[d],
            device_id=partner,
            device_id_type=MESH,
        )

    def grad_part(m):
        return (dot_f32(gk[m], wk[...], NT) + dot_f32(gv[m], wv[...], NT)).astype(bf)

    def out_part(m):
        cols = pl.ds(pl.multiple_of(m * feat, feat), feat)
        return dot_f32(att[...], wo[:, cols]).astype(bf)

    def add(a, b):
        return (a.astype(jnp.float32) + b.astype(jnp.float32)).astype(bf)

    def start_grads(d):
        theirs[d] = grad_part(d * 2 + 1 - core)
        pair_copy(d).start()
        mine[d] = grad_part(d * 2 + core)

    def start_out(d):
        out_theirs[d] = out_part(d * 2 + 1 - core)
        out_pair_copy(d).start()
        out_mine[d] = out_part(d * 2 + core)

    def finish_parts(d):
        out_pair_copy(d).wait()
        out_mine[d] = add(out_mine[d], out_paired[d])
        pair_copy(d).wait()
        mine[d] = add(mine[d], paired[d])

    def target(direction, k):
        j = k // n_dp
        return n_z - 1 - j if direction == 0 else j

    def slot_of(direction, d):
        return d if direction == 0 else jnp.where(d == z - 1, n_z, d)

    def hop(direction, k):
        d = target(direction, k)
        rows = pl.ds(pl.multiple_of((k % n_dp) * chunk, chunk), chunk)
        slot = slot_of(direction, d)
        return pltpu.make_async_remote_copy(
            src_ref=mine.at[d, rows],
            dst_ref=landed.at[slot, rows],
            send_sem=hop_send.at[direction, k],
            recv_sem=hop_recv.at[slot, k % n_dp],
            device_id=(up, down)[direction],
            device_id_type=MESH,
        )

    def hop_arrived(slot, g):
        rows = pl.ds(pl.multiple_of(g * chunk, chunk), chunk)
        pltpu.make_async_remote_copy(
            src_ref=landed.at[slot, rows],
            dst_ref=landed.at[slot, rows],
            send_sem=hop_send.at[0, 0],
            recv_sem=hop_recv.at[slot, g],
            device_id=partner,
            device_id_type=MESH,
        ).wait_recv()
        return rows

    def out_hop(direction, j):
        d = n_z - 1 - j if direction == 0 else j
        slot = slot_of(direction, d)
        return pltpu.make_async_remote_copy(
            src_ref=out_mine.at[d],
            dst_ref=out_landed.at[slot],
            send_sem=out_send.at[direction, j],
            recv_sem=out_recv.at[slot],
            device_id=(up, down)[direction],
            device_id_type=MESH,
        )

    def out_arrived(slot):
        pltpu.make_async_remote_copy(
            src_ref=out_landed.at[slot],
            dst_ref=out_landed.at[slot],
            send_sem=out_send.at[0, 0],
            recv_sem=out_recv.at[slot],
            device_id=partner,
            device_id_type=MESH,
        ).wait_recv()

    sent = (n_z - 1 - z, z)
    from_behind = (has_down, has_up)

    def at_step(s):
        items = []
        for direction in range(2):
            j = s - (z if direction == 0 else n_z - 1 - z)
            d = n_z - 1 - j if direction == 0 else j
            items.append((direction, j, d, jnp.logical_and(j >= 0, j < sent[direction])))
        return items

    at_end = jnp.logical_or(z == 0, z == n_z - 1)

    @pl.when(at_end)
    def _():
        start_grads(n_z - 1 - z)

    weight_copies[-1].wait()

    @pl.when(at_end)
    def _():
        start_out(n_z - 1 - z)

    def step(s, carry):
        items = at_step(s)
        following = at_step(s + 1)
        for direction, j, d, active in items:

            @pl.when(active)
            def _(d=d):
                finish_parts(d)

        for direction, j, d, active in items:

            @pl.when(active)
            def _(direction=direction, j=j, d=d):
                @pl.when(from_behind[direction])
                def _():
                    out_arrived(d)
                    out_mine[d] = add(out_mine[d], out_landed[d])

                out_hop(direction, j).start()

        def each(g, c):
            for direction, j, d, active in items:

                @pl.when(active)
                def _(direction=direction, j=j, d=d):
                    @pl.when(from_behind[direction])
                    def _():
                        rows = hop_arrived(d, g)
                        mine[d, rows, :] = add(mine[d, rows, :], landed[d, rows, :])

                    k = j * n_dp + g

                    @pl.when(k >= 2)
                    def _():
                        hop(direction, k - 2).wait_send()

                    hop(direction, k).start()

            wanted = jnp.logical_and(g == 2, s == n_z - 2)
            part = z
            for direction, j, d, active in following:
                here = g == direction
                wanted = jnp.logical_or(wanted, jnp.logical_and(here, active))
                part = jnp.where(here, d, part)

            @pl.when(wanted)
            def _():
                start_grads(part)
                start_out(part)

            return c

        lax.fori_loop(0, n_dp, each, 0)
        return carry

    lax.fori_loop(0, n_z - 1, step, 0)

    finish_parts(z)

    @pl.when(has_down)
    def _():
        out_arrived(z)
        out_mine[z] = add(out_mine[z], out_landed[z])

    @pl.when(has_up)
    def _():
        out_arrived(n_z)
        out_mine[z] = add(out_mine[z], out_landed[n_z])

    layer_out[...] = out_mine[z]

    def back(g):
        rows = pl.ds(pl.multiple_of(g * chunk, chunk), chunk)
        return pltpu.make_async_remote_copy(
            src_ref=mine.at[z, rows],
            dst_ref=returned.at[dp],
            send_sem=a2a_send.at[g],
            recv_sem=a2a_recv.at[dp],
            device_id={"dp": g},
            device_id_type=MESH,
        )

    def back_arrived(g):
        rows = pl.ds(pl.multiple_of(g * chunk, chunk), chunk)
        pltpu.make_async_remote_copy(
            src_ref=mine.at[z, rows],
            dst_ref=returned.at[g],
            send_sem=a2a_send.at[g],
            recv_sem=a2a_recv.at[g],
            device_id={"dp": g},
            device_id_type=MESH,
        ).wait_recv()

    own_rows = pl.ds(pl.multiple_of(dp * chunk, chunk), chunk)
    own_copy = pltpu.make_async_copy(mine.at[z, own_rows], returned.at[dp], own_sem)

    def last(g, c):
        rows = pl.ds(pl.multiple_of(g * chunk, chunk), chunk)

        @pl.when(has_down)
        def _():
            hop_arrived(z, g)
            mine[z, rows, :] = add(mine[z, rows, :], landed[z, rows, :])

        @pl.when(has_up)
        def _():
            hop_arrived(n_z, g)
            mine[z, rows, :] = add(mine[z, rows, :], landed[n_z, rows, :])

        @pl.when(g != dp)
        def _():
            back(g).start()

        @pl.when(g == dp)
        def _():
            own_copy.start()

        return c

    lax.fori_loop(0, n_dp, last, 0)
    own_copy.wait()

    def finish(g, c):
        @pl.when(g != dp)
        def _():
            back(g).wait_send()
            back_arrived(g)

        return c

    lax.fori_loop(0, n_dp, finish, 0)

    for direction in range(2):

        @pl.when(sent[direction] > 0)
        def _(direction=direction):
            count = sent[direction] * n_dp
            hop(direction, count - 2).wait_send()
            hop(direction, count - 1).wait_send()

        def drain(j, c, direction=direction):
            @pl.when(j < sent[direction])
            def _():
                out_hop(direction, j).wait_send()

            return c

        lax.fori_loop(0, n_z - 1, drain, 0)


def backward(att, gk, gv, w_key, w_value, w_out, n_dp, n_mp):
    tokens = att.shape[0]
    shard = gk.shape[1]
    enc = w_key.shape[0]
    feat = w_out.shape[1] // n_mp
    n_z = n_mp // 2
    bf = jnp.bfloat16
    hbm = pl.BlockSpec(memory_space=pl.ANY)
    vm = pl.BlockSpec(memory_space=pltpu.VMEM)
    dma = pltpu.SemaphoreType.DMA
    return pl.pallas_call(
        functools.partial(backward_kernel, n_dp, n_mp),
        out_shape=(
            jax.ShapeDtypeStruct((tokens, feat), bf),
            jax.ShapeDtypeStruct((n_dp, shard // n_dp, enc), bf),
        ),
        in_specs=[vm, hbm, hbm, hbm, hbm, hbm],
        out_specs=(vm, hbm),
        scratch_shapes=[
            pltpu.VMEM(gk.shape, bf),
            pltpu.VMEM(gv.shape, bf),
            pltpu.VMEM(w_key.shape, bf),
            pltpu.VMEM(w_value.shape, bf),
            pltpu.VMEM(w_out.shape, bf),
            pltpu.VMEM((n_z, shard, enc), bf),
            pltpu.VMEM((n_z, shard, enc), bf),
            pltpu.VMEM((n_z, shard, enc), bf),
            pltpu.VMEM((n_z + 1, shard, enc), bf),
            pltpu.VMEM((n_z, tokens, feat), bf),
            pltpu.VMEM((n_z, tokens, feat), bf),
            pltpu.VMEM((n_z, tokens, feat), bf),
            pltpu.VMEM((n_z + 1, tokens, feat), bf),
            dma((5,)),
            dma((n_z,)),
            dma((n_z,)),
            dma((n_z,)),
            dma((n_z,)),
            dma((2, n_z * n_dp)),
            dma((n_z + 1, n_dp)),
            dma((2, n_z)),
            dma((n_z + 1,)),
            dma((n_dp,)),
            dma((n_dp,)),
            dma,
        ],
        compiler_params=pltpu.CompilerParams(
            collective_id=1, has_side_effects=True, vmem_limit_bytes=VMEM_LIMIT
        ),
        name="grads_scatter",
    )(att, gk, gv, w_key, w_value, w_out)


def per_device(hidden_in, out_grad, neighbours, counts, slot_owner, w_query, w_key, w_value, w_out):
    groups = lax.axis_size("dp")
    n_mp = lax.axis_size("mp")
    spans = counts.shape[0]
    slots_group = spans * MAXN
    src_slots = slot_owner.shape[0]
    capacity = src_slots // groups
    rows_dev = neighbours.shape[1]
    enc_width = neighbours.shape[2]
    slot_order = jnp.arange(src_slots, dtype=jnp.int32)
    dest_group = jnp.where(slot_owner >= 0, slot_owner // slots_group, -1)
    earlier = (dest_group[None, :] == dest_group[:, None]) & (
        slot_order[None, :] < slot_order[:, None]
    )
    rank_in = jnp.sum(earlier.astype(jnp.int32), axis=1)
    position = jnp.where(slot_owner >= 0, dest_group * capacity + rank_in, -1)
    picked = position[None, :] == slot_order[:, None]
    source = jnp.sum(jnp.where(picked, slot_order[None, :], 0), axis=1)
    send_rows = neighbours.at[source].get(mode="promise_in_bounds")
    send_rows = send_rows.reshape(groups, capacity * rows_dev, enc_width)
    send_tags = jnp.sum(
        jnp.where(picked, slot_owner[None, :] + 1, 0), axis=1
    ).reshape(groups, capacity) - 1
    counts_rows = jnp.broadcast_to(counts[:, None], (spans, hidden_in.shape[0]))
    attended, grad_keys, grad_values = forward(
        hidden_in,
        out_grad,
        send_rows,
        send_tags,
        counts_rows,
        w_query,
        w_key,
        w_value,
        w_out,
        groups,
        n_mp,
    )
    layer_out, returned = backward(
        attended, grad_keys, grad_values, w_key, w_value, w_out, groups, n_mp
    )
    returned = returned.reshape(src_slots, rows_dev, enc_width)
    neighbour_grad = jnp.where(
        (slot_owner >= 0)[:, None, None],
        jnp.take(returned, jnp.maximum(position, 0), axis=0),
        jnp.zeros((), jnp.bfloat16),
    )
    return (layer_out, neighbour_grad)


def solution(mesh):
    return jax.shard_map(
        per_device,
        mesh=mesh,
        in_specs=(
            P("dp", "mp"),
            P("dp", "mp"),
            P("dp", "mp", None),
            P("dp"),
            P("dp"),
            P(None, "mp"),
            P(None, "mp"),
            P(None, "mp"),
            P("mp", None),
        ),
        out_specs=(P("dp", "mp"), P("dp", "mp", None)),
        check_vma=False,
    )
```
